32 devices in a mesh: groups: 2 (over x), grid: 8 (over z, y), layer: 2 (over core).
Axes of the slice: x: 2, y: 2, z: 4, core: 2. Of those that a mesh axis runs over, the one named last changes fastest.
Arguments:
- leaf_rhs: float32 [384, 128, 256], P(('groups', 'grid', 'layer')), parts along dimension 0, may hold values from -6 to 6
- leaf_lower_inverse: float32 [384, 128, 128], P(('groups', 'grid', 'layer')), parts along dimension 0, as said below
- leaf_upper_inverse: float32 [384, 128, 128], P(('groups', 'grid', 'layer')), parts along dimension 0, as said below
- leaf_lower: float32 [384, 4, 128, 128], P(('groups', 'grid', 'layer')), parts along dimension 0, may hold values from -0.109375 to 0.109375
- leaf_upper: float32 [384, 4, 128, 128], P(('groups', 'grid', 'layer')), parts along dimension 0, may hold values from -0.25 to 0.25
- leaf_rows: int32 [384, 4], P(('groups', 'grid', 'layer')), parts along dimension 0, may hold values from 0 to 6, as said below
- separator_right_sides: float32 [32, 128, 256], P(('groups', 'grid', 'layer')), parts along dimension 0, may hold values from -6 to 6
- separator_lower_inverse: float32 [32, 128, 128], P(('groups', 'grid', 'layer')), parts along dimension 0, as said below
- separator_upper_inverse: float32 [32, 128, 128], P(('groups', 'grid', 'layer')), parts along dimension 0, as said below
- separator_lower_blocks: float32 [32, 3, 128, 128], P(('groups', 'grid', 'layer')), parts along dimension 0, may hold values from -0.21875 to 0.21875
- sep_upper: float32 [32, 3, 128, 128], P(('groups', 'grid', 'layer')), parts along dimension 0, may hold values from -0.3125 to 0.3125
- sep_rows: int32 [32, 3], P(('groups', 'grid', 'layer')), parts along dimension 0, may hold values from 0 to 3, as said below
- root_rhs: float32 [8, 128, 256], P('groups'), parts along dimension 0, may hold values from -6 to 6
- root_lower_inverse: float32 [8, 128, 128], P('groups'), parts along dimension 0, as said below
- root_upper_inverse: float32 [8, 128, 128], P('groups'), parts along dimension 0, as said below
- root_lower: float32 [1024, 512], P('groups'), parts along dimension 0, may hold values from -0.25 to 0.25
- root_upper: float32 [1024, 512], P('groups'), parts along dimension 0, may hold values from -0.25 to 0.25
Outputs:
- leaf_sol: float32 [384, 128, 256], P(('groups', 'grid', 'layer')), parts along dimension 0
- separator_solution_rows: float32 [32, 128, 256], P(('groups', 'grid', 'layer')), parts along dimension 0
- root_sol: float32 [8, 128, 256], P('groups'), parts along dimension 0
The draws below stay inside these ranges and needn't reach their ends.
There are 2 independent parts, one for each index of `groups`. The reference program is written for one: setup_inputs(seed, part) draws one part's arguments, and reference() takes and returns one part's arrays. A program takes and returns all parts, laid end to end along the dimension named above; each array names one. Nothing has to cross between parts.
Inputs may be any that keep to these rules, and one draw needn't show every extreme that they name: `leaf_rows`: in each row the first value is 0, 1 or 2 and the other 3 values are different values of 3 to 6; among the 12 leaves of one home each of 0, 1 and 2 stands in the first column. `sep_rows`: each row names 3 different values. `leaf_lower_inverse`: zero above the diagonal; diagonal entries between 0.5 and 1.5. `leaf_upper_inverse`: zero below the diagonal; diagonal entries between 0.5 and 1.5. `separator_lower_inverse`: zero above the diagonal; diagonal entries between 0.5 and 1.5. `separator_upper_inverse`: zero below the diagonal; diagonal entries between 0.5 and 1.5. `root_lower_inverse`: zero above the diagonal; diagonal entries between 0.5 and 1.5. `root_upper_inverse`: zero below the diagonal; diagonal entries between 0.5 and 1.5.
All inputs are finite; a program needn't handle non-finite values.
Results may differ from the reference program's by a relative error of at most 0.0001.
Values sent between devices are 32-bit elements; how exact they have to be, the bound alone decides.
No kernel may reach another device: no remote copies, remote signals or barrier semaphores. Data moves between devices by JAX's collectives and lax.ppermute only.
A program may use at most 128 MiB of HBM per device.

```python
import math
import jax
import jax.numpy as jnp
from jax import lax

W = 128
R = 256
LEAF_DEV = 12
LEAF_LINKS = 4
SEP_LINKS = 3
ROOTS = 4
LEAVES = 192
SEPARATOR_NODES = 16
N_GRID = 8
N_LAYER = 2


def inverse_blocks(noise, diag_key, upper):
    count = noise.shape[0]
    size = noise.shape[1]
    lower = jnp.tril(jnp.clip(noise, -4.0, 4.0) * (0.6 / math.sqrt(size)), -1)
    diagonal = jax.random.uniform(diag_key, (count, size), jnp.float32, 0.5, 1.5)
    blocks = lower + diagonal[:, :, None] * jnp.eye(size, dtype=jnp.float32)[None]
    if upper:
        return jnp.swapaxes(blocks, 1, 2)
    return blocks


def distinct_links(key, total_rows, choices, links):
    score_key, bias_key = jax.random.split(key)
    scores = jax.random.randint(score_key, (total_rows, choices), 0, 16384, dtype=jnp.int32)
    favour = jax.random.randint(bias_key, (choices,), 0, 8192, dtype=jnp.int32)
    column = jnp.arange(choices, dtype=jnp.int32)
    forced = (jnp.arange(total_rows, dtype=jnp.int32)[:, None] % choices == column[None, :]).astype(jnp.int32)
    ranking = (scores + favour[None, :] + forced * 65536) * choices + column[None, :]
    _, picked = lax.top_k(ranking, links)
    return picked.astype(jnp.int32)


def draw_leaf_rows(key, part):
    key = jax.random.fold_in(key, 21)
    bit_key, place_key, root_key = jax.random.split(key, 3)
    homes = LEAVES // LEAF_DEV
    parents = jax.random.randint(bit_key, (homes, LEAF_DEV), 0, 3, dtype=jnp.int32)
    first = jax.random.randint(place_key, (homes, 1), 0, LEAF_DEV, dtype=jnp.int32)
    local = jnp.arange(LEAF_DEV, dtype=jnp.int32)[None, :]
    parents = jnp.where(local == first, 0, jnp.where(local == (first + 1) % LEAF_DEV, 1, jnp.where(local == (first + 2) % LEAF_DEV, 2, parents)))
    roots = distinct_links(root_key, LEAVES, ROOTS, LEAF_LINKS - 1) + 3
    return jnp.concatenate([parents.reshape(LEAVES, 1), roots], axis=1).astype(jnp.int32)


def draw_sep_rows(key, part):
    key = jax.random.fold_in(key, 22)
    return distinct_links(key, SEPARATOR_NODES, ROOTS, SEP_LINKS)


def draw_leaf_lower_inverse(key, part):
    key = jax.random.fold_in(key, 11)
    noise_key, diag_key = jax.random.split(key)
    noise = jax.random.normal(noise_key, (LEAVES, W, W), jnp.float32)
    return inverse_blocks(noise, diag_key, False)


def draw_leaf_upper_inverse(key, part):
    key = jax.random.fold_in(key, 12)
    noise_key, diag_key = jax.random.split(key)
    noise = jax.random.normal(noise_key, (LEAVES, W, W), jnp.float32)
    return inverse_blocks(noise, diag_key, True)


def draw_separator_lower_inverse(key, part):
    key = jax.random.fold_in(key, 13)
    noise_key, diag_key = jax.random.split(key)
    noise = jax.random.normal(noise_key, (SEPARATOR_NODES, W, W), jnp.float32)
    return inverse_blocks(noise, diag_key, False)


def draw_separator_upper_inverse(key, part):
    key = jax.random.fold_in(key, 14)
    noise_key, diag_key = jax.random.split(key)
    noise = jax.random.normal(noise_key, (SEPARATOR_NODES, W, W), jnp.float32)
    return inverse_blocks(noise, diag_key, True)


def draw_root_lower_inverse(key, part):
    key = jax.random.fold_in(key, 15)
    noise_key, diag_key = jax.random.split(key)
    noise = jax.random.normal(noise_key, (ROOTS, W, W), jnp.float32)
    return inverse_blocks(noise, diag_key, False)


def draw_root_upper_inverse(key, part):
    key = jax.random.fold_in(key, 16)
    noise_key, diag_key = jax.random.split(key)
    noise = jax.random.normal(noise_key, (ROOTS, W, W), jnp.float32)
    return inverse_blocks(noise, diag_key, True)


def level_of(key, extent, pieces, smallest, high):
    loudness = 1.0
    for position, parts in pieces:
        steps = jax.random.uniform(jax.random.fold_in(jax.random.fold_in(key, 6), position), (parts,), jnp.float32, smallest / len(pieces), high / len(pieces))
        loudness = loudness * jnp.repeat(jnp.exp(steps), extent[position] // parts).reshape((-1,) + (1,) * (len(extent) - 1 - position))
    return loudness


def normal_values(rng, dims, deviation, reach, cuts=(), kind=jnp.bfloat16):
    entries = deviation * jax.random.normal(rng, dims, jnp.float32)
    if cuts:
        entries = entries * level_of(rng, dims, cuts, -0.22, 0.18)
    return jnp.clip(entries, -reach, reach).astype(kind)


def setup_inputs(seed: int = 0, part: int = 0) -> dict:
    streams_of = jax.random.split(jax.random.key(seed), 18)
    part_keys = jax.random.split(jax.random.fold_in(streams_of[17], part), 18)
    return {
        "leaf_rhs": normal_values(part_keys[0], (LEAVES, W, R), 1.0, 6.0, ((0, 16),), jnp.float32),
        "leaf_lower_inverse": draw_leaf_lower_inverse(jax.random.fold_in(jax.random.fold_in(streams_of[17], part), 71), part),
        "leaf_upper_inverse": draw_leaf_upper_inverse(jax.random.fold_in(jax.random.fold_in(streams_of[17], part), 71), part),
        "leaf_lower": normal_values(part_keys[3], (LEAVES, LEAF_LINKS, W, W), (W * LEAF_DEV * LEAF_LINKS // 2) ** -0.5, 0.109375, ((0, 16),), jnp.float32),
        "leaf_upper": normal_values(part_keys[4], (LEAVES, LEAF_LINKS, W, W), (W * LEAF_LINKS) ** -0.5, 0.25, ((0, 16),), jnp.float32),
        "leaf_rows": draw_leaf_rows(jax.random.fold_in(jax.random.fold_in(streams_of[17], part), 71), part),
        "separator_right_sides": normal_values(part_keys[6], (SEPARATOR_NODES, W, R), 1.0, 6.0, ((0, 16),), jnp.float32),
        "separator_lower_inverse": draw_separator_lower_inverse(jax.random.fold_in(jax.random.fold_in(streams_of[17], part), 71), part),
        "separator_upper_inverse": draw_separator_upper_inverse(jax.random.fold_in(jax.random.fold_in(streams_of[17], part), 71), part),
        "separator_lower_blocks": normal_values(part_keys[9], (SEPARATOR_NODES, SEP_LINKS, W, W), (W * SEP_LINKS * 2) ** -0.5, 0.21875, ((0, 16),), jnp.float32),
        "sep_upper": normal_values(part_keys[10], (SEPARATOR_NODES, SEP_LINKS, W, W), (W * SEP_LINKS) ** -0.5, 0.3125, ((0, 16),), jnp.float32),
        "sep_rows": draw_sep_rows(jax.random.fold_in(jax.random.fold_in(streams_of[17], part), 71), part),
        "root_rhs": normal_values(part_keys[12], (ROOTS, W, R), 1.0, 6.0, (), jnp.float32),
        "root_lower_inverse": draw_root_lower_inverse(jax.random.fold_in(jax.random.fold_in(streams_of[17], part), 71), part),
        "root_upper_inverse": draw_root_upper_inverse(jax.random.fold_in(jax.random.fold_in(streams_of[17], part), 71), part),
        "root_lower": normal_values(part_keys[15], (ROOTS * W, ROOTS * W), (ROOTS * W) ** -0.5, 0.25, (), jnp.float32),
        "root_upper": normal_values(part_keys[16], (ROOTS * W, ROOTS * W), (ROOTS * W) ** -0.5, 0.25, (), jnp.float32),
    }


precise_mode = lax.Precision.HIGHEST


def reference(leaf_rhs, leaf_lower_inverse, leaf_upper_inverse, leaf_lower, leaf_upper, leaf_rows, separator_right_sides, separator_lower_inverse, separator_upper_inverse, separator_lower_blocks, sep_upper, sep_rows, root_rhs, root_lower_inverse, root_upper_inverse, root_lower, root_upper):
    home = jnp.arange(LEAVES, dtype=jnp.int32) // LEAF_DEV
    leaf_layer = home % N_LAYER
    leaf_grid = home // N_LAYER
    offsets = jnp.where(leaf_rows == 2, N_GRID // 2, leaf_rows).astype(jnp.int32)
    parent_grid = (leaf_grid[:, None] - offsets) % N_GRID
    slot_index = jnp.where(leaf_rows < 3, parent_grid * N_LAYER + leaf_layer[:, None], SEPARATOR_NODES + leaf_rows - 3).astype(jnp.int32)
    leaf_solved = jnp.einsum("kab,kbr->kar", leaf_lower_inverse, leaf_rhs, precision=precise_mode)
    leaf_terms = jnp.einsum("knab,kbr->knar", leaf_lower, leaf_solved, precision=precise_mode)
    upper_partial_sums = jax.ops.segment_sum(leaf_terms.reshape(LEAVES * LEAF_LINKS, W, R), slot_index.reshape(-1), num_segments=SEPARATOR_NODES + ROOTS)
    separator_solved_rows = jnp.einsum("pdz,pzt->pdt", separator_lower_inverse, separator_right_sides - upper_partial_sums[:SEPARATOR_NODES], precision=precise_mode)
    separator_update_terms = jnp.einsum("jzpi,jik->jzpk", separator_lower_blocks, separator_solved_rows, precision=precise_mode)
    root_sums = upper_partial_sums[SEPARATOR_NODES:] + jax.ops.segment_sum(separator_update_terms.reshape(SEPARATOR_NODES * SEP_LINKS, W, R), sep_rows.reshape(-1), num_segments=ROOTS)
    pending = root_rhs - root_sums

    def forward_step(index, solved):
        row_block = lax.dynamic_slice_in_dim(root_lower, index * W, W, 0)
        earlier = jnp.dot(row_block, solved.reshape(ROOTS * W, R), precision=precise_mode)
        rest = lax.dynamic_slice_in_dim(pending, index, 1, 0)[0] - earlier
        inverse = lax.dynamic_slice_in_dim(root_lower_inverse, index, 1, 0)[0]
        value = jnp.dot(inverse, rest, precision=precise_mode)
        return lax.dynamic_update_slice_in_dim(solved, value[None], index, 0)

    root_solved = lax.fori_loop(0, ROOTS, forward_step, jnp.zeros((ROOTS, W, R), jnp.float32))

    def backward_step(counter, solution):
        index = ROOTS - 1 - counter
        row_block = lax.dynamic_slice_in_dim(root_upper, index * W, W, 0)
        later = jnp.dot(row_block, solution.reshape(ROOTS * W, R), precision=precise_mode)
        rest = lax.dynamic_slice_in_dim(root_solved, index, 1, 0)[0] - later
        inverse = lax.dynamic_slice_in_dim(root_upper_inverse, index, 1, 0)[0]
        value = jnp.dot(inverse, rest, precision=precise_mode)
        return lax.dynamic_update_slice_in_dim(solution, value[None], index, 0)

    root_sol = lax.fori_loop(0, ROOTS, backward_step, jnp.zeros((ROOTS, W, R), jnp.float32))
    linked = jnp.take(root_sol, sep_rows, axis=0)
    separator_remainder = separator_solved_rows - jnp.einsum("snab,snbr->sar", sep_upper, linked, precision=precise_mode)
    separator_solution_rows = jnp.einsum("pdz,pzt->pdt", separator_upper_inverse, separator_remainder, precision=precise_mode)
    solutions = jnp.concatenate([separator_solution_rows, root_sol], axis=0)
    picked = jnp.take(solutions, slot_index, axis=0)
    leaf_rest = leaf_solved - jnp.einsum("knab,knbr->kar", leaf_upper, picked, precision=precise_mode)
    leaf_sol = jnp.einsum("kab,kbr->kar", leaf_upper_inverse, leaf_rest, precision=precise_mode)
    return leaf_sol, separator_solution_rows, root_sol
```

```python
import functools

import jax
import jax.numpy as jnp
from jax import lax
from jax.experimental import pallas as pl
from jax.experimental.pallas import tpu as pltpu
from jax.sharding import PartitionSpec as P

VMEM = pltpu.VMEM
SMEM = pltpu.SMEM
F32 = jnp.float32
BF16 = jnp.bfloat16


def parts_of(x):
    high = x.astype(BF16)
    low = (x - high.astype(F32)).astype(BF16)
    return high, low


def as_left(x):
    high, low = parts_of(x)
    count = x.shape[1] // 128
    pieces = [slice(j * 128, j * 128 + 128) for j in range(count)]
    top = jnp.concatenate([high[:, s] for s in pieces for _ in range(2)], axis=1)
    bottom = jnp.concatenate([low[:, s] for s in pieces for _ in range(2)], axis=1)
    return jnp.concatenate([top, bottom], axis=0)


def as_right(x):
    high, low = parts_of(x)
    count = x.shape[0] // 128
    pieces = [slice(j * 128, j * 128 + 128) for j in range(count)]
    return jnp.concatenate([y[s] for s in pieces for y in (high, low)], axis=0)


def left_times(left, right):
    both = jnp.dot(left, right, preferred_element_type=F32)
    rows = left.shape[0] // 2
    return both[:rows] + both[rows:]


def times(a, b):
    return left_times(as_left(a), as_right(b))


def cost(units):
    return pl.CostEstimate(
        flops=units * 2 * 128 * 128 * 256 * 3, bytes_accessed=units * 65536, transcendentals=0
    )


def forward_leaf_kernel(rows, rhs, inverse, first, solved, pending):
    step = pl.program_id(0)

    @pl.when(step == 0)
    def _():
        pending[...] = jnp.zeros_like(pending)

    batch = rhs.shape[0]
    for i in range(batch):
        value = times(inverse[i], rhs[i])
        solved[i] = value
        slot = rows[(step * batch + i) * 4]
        pending[slot] += times(first[i, 0], value)


def root_terms_kernel(rows, one, two, three, solved, after, pending):
    step = pl.program_id(0)

    @pl.when(step == 0)
    def _():
        pending[...] = jnp.zeros_like(pending)

    batch = solved.shape[0]
    for i in range(batch):
        blocks = jnp.concatenate([one[i, 0], two[i, 0], three[i, 0]], axis=0)
        terms = times(blocks, solved[i])
        for n in range(3):
            slot = rows[(step * batch + i) * 4 + n + 1] - 3
            pending[slot] += terms[n * 128 : n * 128 + 128]


def operators_kernel(lower_inverse, upper_inverse, lower, upper, after, forward, backward):
    count = lower_inverse.shape[0]
    w = lower_inverse.shape[1]
    forward[...] = jnp.zeros_like(forward)
    backward[...] = jnp.zeros_like(backward)
    for r in range(count):
        here = slice(r * w, r * w + w)
        forward[here, here] = lower_inverse[r]
        if r > 0:
            done = slice(0, r * w)
            inner = times(lower[here, done], forward[done, done])
            forward[here, done] = -times(lower_inverse[r], inner)
    for r in reversed(range(count)):
        here = slice(r * w, r * w + w)
        backward[here, here] = upper_inverse[r]
        if r < count - 1:
            done = slice((r + 1) * w, count * w)
            inner = times(upper[here, done], backward[done, done])
            backward[here, done] = -times(upper_inverse[r], inner)


def separator_kernel(
    rows, core, rhs, inverse, blocks, own, near, far, root_pending, solved, mine, theirs, sums
):
    value = times(inverse[0], rhs[0] - own[...] - near[...] - far[...])
    solved[...] = value
    terms = times(blocks[0].reshape(3 * 128, 128), value)
    sums[...] = root_pending[...]
    for n in range(3):
        sums[rows[n]] += terms[n * 128 : n * 128 + 128]
    total = sums[...]
    first_half, second_half = total[:, :, :128], total[:, :, 128:]
    is_first = core[0] == 0

    @pl.when(is_first)
    def _():
        mine[...] = first_half
        theirs[...] = second_half

    @pl.when(jnp.logical_not(is_first))
    def _():
        mine[...] = second_half
        theirs[...] = first_half


def root_kernel(place, rhs, forward, backward, own, one, two, three, out, pending):
    count, w = rhs.shape[0], rhs.shape[1]
    position = place[0]
    is_first = place[1] == 0
    for j, piece in enumerate((own, one, two, three)):
        root = position ^ j
        right = rhs[root]
        right = jnp.where(is_first, right[:, :128], right[:, 128:])
        pending[pl.ds(pl.multiple_of(root * w, w), w), :] = right - piece[...]
    solved = times(forward[...], pending[...])
    solution = times(backward[...], solved)
    out[...] = solution.reshape(count, w, 128)


def separator_back_kernel(rows, core, mine, theirs, upper, inverse, solved, root_sol, out):
    is_first = core[0] == 0

    @pl.when(is_first)
    def _():
        root_sol[:, :, :128] = mine[...]
        root_sol[:, :, 128:] = theirs[...]

    @pl.when(jnp.logical_not(is_first))
    def _():
        root_sol[:, :, :128] = theirs[...]
        root_sol[:, :, 128:] = mine[...]

    blocks = jnp.concatenate([upper[0, n] for n in range(3)], axis=1)
    linked = jnp.concatenate([root_sol[rows[n]] for n in range(3)], axis=0)
    out[0] = times(inverse[0], solved[...] - times(blocks, linked))


def leaf_root_part_kernel(rows, one, two, three, solved, root_sol, rest):
    step = pl.program_id(0)
    batch = solved.shape[0]
    for i in range(batch):
        base = (step * batch + i) * 4
        blocks = jnp.concatenate([one[i, 0], two[i, 0], three[i, 0]], axis=1)
        linked = jnp.concatenate([root_sol[rows[base + n] - 3] for n in (1, 2, 3)], axis=0)
        rest[i] = solved[i] - times(blocks, linked)


def leaf_final_kernel(rows, first, inverse, rest, own, near, far, out, seps):
    step = pl.program_id(0)

    @pl.when(step == 0)
    def _():
        seps[0] = own[0]
        seps[1] = near[...]
        seps[2] = far[...]

    batch = rest.shape[0]
    for i in range(batch):
        slot = rows[(step * batch + i) * 4]
        out[i] = times(inverse[i], rest[i] - times(first[i, 0], seps[slot]))


def whole(memory=VMEM):
    return pl.BlockSpec(memory_space=memory)


ANY = pl.BlockSpec(memory_space=pl.ANY)


def leafwise(batch, *tail):
    return pl.BlockSpec((batch,) + tail, lambda k: (k,) + (0,) * len(tail))


def link(batch, n, w):
    return pl.BlockSpec((batch, 1, w, w), lambda k: (k, n, 0, 0))


def kept(*shape):
    return pl.BlockSpec(shape, lambda k: (0,) * len(shape))


def per_device(
    leaf_rhs,
    leaf_lower_inverse,
    leaf_upper_inverse,
    leaf_lower,
    leaf_upper,
    leaf_rows,
    separator_right_sides,
    separator_lower_inverse,
    separator_upper_inverse,
    separator_lower_blocks,
    sep_upper,
    sep_rows,
    root_rhs,
    root_lower_inverse,
    root_upper_inverse,
    root_lower,
    root_upper,
):
    peers = lax.axis_size("grid")
    leaves, w, columns = leaf_rhs.shape
    roots = root_rhs.shape[0]
    half = columns // 2
    batch = 3
    steps = leaves // batch
    position = lax.axis_index("grid") % 4
    core = lax.axis_index("layer")
    core_ref = core.astype(jnp.int32).reshape(1)
    place = jnp.stack([position, core]).astype(jnp.int32)
    leaf_links = leaf_rows.reshape(-1)
    sep_links = sep_rows.reshape(-1)

    def shifted(x, by):
        return lax.ppermute(x, "grid", [(i, (i + by) % peers) for i in range(peers)])

    def crossed(x, bit):
        return lax.ppermute(x, "grid", [(i, i ^ bit) for i in range(peers)])

    def swapped(x):
        return lax.ppermute(x, "layer", [(0, 1), (1, 0)])

    shape = jax.ShapeDtypeStruct

    leaf_solved, pending = pl.pallas_call(
        forward_leaf_kernel,
        grid=(steps,),
        in_specs=[
            whole(SMEM),
            leafwise(batch, w, columns),
            leafwise(batch, w, w),
            link(batch, 0, w),
        ],
        out_specs=[leafwise(batch, w, columns), kept(3, w, columns)],
        out_shape=[shape((leaves, w, columns), F32), shape((3, w, columns), F32)],
        cost_estimate=cost(24),
        name="leaf_forward",
    )(leaf_links, leaf_rhs, leaf_lower_inverse, leaf_lower)

    near_sum = shifted(pending[1], -1)
    far_sum = shifted(pending[2], -(peers // 2))

    root_pending = pl.pallas_call(
        root_terms_kernel,
        grid=(steps,),
        in_specs=[
            whole(SMEM),
            link(batch, 1, w),
            link(batch, 2, w),
            link(batch, 3, w),
            leafwise(batch, w, columns),
            ANY,
        ],
        out_specs=kept(roots, w, columns),
        out_shape=shape((roots, w, columns), F32),
        cost_estimate=cost(36),
        name="root_terms",
    )(leaf_links, leaf_lower, leaf_lower, leaf_lower, leaf_solved, pending)

    forward, backward = pl.pallas_call(
        operators_kernel,
        in_specs=[whole(), whole(), whole(), whole(), ANY],
        out_specs=[whole(), whole()],
        out_shape=[shape((roots * w, roots * w), F32)] * 2,
        cost_estimate=cost(32),
        name="root_operators",
    )(root_lower_inverse, root_upper_inverse, root_lower, root_upper, pending)

    sep_solved, mine, theirs = pl.pallas_call(
        separator_kernel,
        in_specs=[whole(SMEM), whole(SMEM)] + [whole()] * 7,
        out_specs=[whole()] * 3,
        out_shape=[
            shape((w, columns), F32),
            shape((roots, w, half), F32),
            shape((roots, w, half), F32),
        ],
        scratch_shapes=[VMEM((roots, w, columns), F32)],
        cost_estimate=cost(4),
        name="separator_forward",
    )(
        sep_links,
        core_ref,
        separator_right_sides,
        separator_lower_inverse,
        separator_lower_blocks,
        pending[0],
        near_sum,
        far_sum,
        root_pending,
    )

    both = mine + swapped(theirs)
    total = lax.dynamic_index_in_dim(both, position, 0, keepdims=False)
    for j in (1, 2, 3):
        total = total + crossed(
            lax.dynamic_index_in_dim(both, position ^ j, 0, keepdims=False), j
        )
    bit = 4
    while bit < peers:
        total = total + crossed(total, bit)
        bit *= 2
    others = [crossed(total, j) for j in (1, 2, 3)]

    solution_half = pl.pallas_call(
        root_kernel,
        in_specs=[whole(SMEM)] + [whole()] * 7,
        out_specs=whole(),
        out_shape=shape((roots, w, half), F32),
        scratch_shapes=[VMEM((roots * w, half), F32)],
        cost_estimate=cost(16),
        name="root_solve",
    )(place, root_rhs, forward, backward, total, *others)

    other_half = swapped(solution_half)

    root_sol, separator_solution_rows = pl.pallas_call(
        separator_back_kernel,
        in_specs=[whole(SMEM), whole(SMEM)] + [whole()] * 5,
        out_specs=[whole()] * 2,
        out_shape=[shape((roots, w, columns), F32), shape((1, w, columns), F32)],
        cost_estimate=cost(4),
        name="separator_backward",
    )(
        sep_links,
        core_ref,
        solution_half,
        other_half,
        sep_upper,
        separator_upper_inverse,
        sep_solved,
    )

    near_rows = shifted(separator_solution_rows[0], 1)
    far_rows = shifted(separator_solution_rows[0], peers // 2)

    leaf_rest = pl.pallas_call(
        leaf_root_part_kernel,
        grid=(steps,),
        in_specs=[
            whole(SMEM),
            link(batch, 1, w),
            link(batch, 2, w),
            link(batch, 3, w),
            leafwise(batch, w, columns),
            kept(roots, w, columns),
        ],
        out_specs=leafwise(batch, w, columns),
        out_shape=shape((leaves, w, columns), F32),
        cost_estimate=cost(36),
        name="leaf_root_part",
    )(leaf_links, leaf_upper, leaf_upper, leaf_upper, leaf_solved, root_sol)

    leaf_sol = pl.pallas_call(
        leaf_final_kernel,
        grid=(steps,),
        in_specs=[
            whole(SMEM),
            link(batch, 0, w),
            leafwise(batch, w, w),
            leafwise(batch, w, columns),
            kept(1, w, columns),
            kept(w, columns),
            kept(w, columns),
        ],
        out_specs=leafwise(batch, w, columns),
        out_shape=shape((leaves, w, columns), F32),
        scratch_shapes=[VMEM((3, w, columns), F32)],
        cost_estimate=cost(24),
        name="leaf_backward",
    )(
        leaf_links,
        leaf_upper,
        leaf_upper_inverse,
        leaf_rest,
        separator_solution_rows,
        near_rows,
        far_rows,
    )
    return (leaf_sol, separator_solution_rows, root_sol)


def solution(mesh):
    by_device = P(("groups", "grid", "layer"))
    by_group = P("groups")
    return jax.shard_map(
        per_device,
        mesh=mesh,
        in_specs=(by_device,) * 12 + (by_group,) * 5,
        out_specs=(by_device, by_device, by_group),
        check_vma=False,
    )
```

```python
import functools

import jax
import jax.numpy as jnp
from jax import lax
from jax.experimental import pallas as pl
from jax.experimental.pallas import tpu as pltpu
from jax.sharding import PartitionSpec as P

VMEM = pltpu.VMEM
SMEM = pltpu.SMEM
F32 = jnp.float32
BF16 = jnp.bfloat16


def parts_of(x):
    high = x.astype(BF16)
    low = (x - high.astype(F32)).astype(BF16)
    return high, low


def as_left(x):
    high, low = parts_of(x)
    count = x.shape[1] // 128
    pieces = [slice(j * 128, j * 128 + 128) for j in range(count)]
    top = jnp.concatenate([high[:, s] for s in pieces for _ in range(2)], axis=1)
    bottom = jnp.concatenate([low[:, s] for s in pieces for _ in range(2)], axis=1)
    return jnp.concatenate([top, bottom], axis=0)


def as_right(x):
    high, low = parts_of(x)
    count = x.shape[0] // 128
    pieces = [slice(j * 128, j * 128 + 128) for j in range(count)]
    return jnp.concatenate([y[s] for s in pieces for y in (high, low)], axis=0)


def left_times(left, right):
    both = jnp.dot(left, right, preferred_element_type=F32)
    rows = left.shape[0] // 2
    return both[:rows] + both[rows:]


def times(a, b):
    return left_times(as_left(a), as_right(b))


def cost(microseconds):
    return pl.CostEstimate(
        flops=int(microseconds * 1e9),
        bytes_accessed=int(microseconds * 3e6),
        transcendentals=0,
    )


def forward_leaf_kernel(links, rhs, inverse, first, solved, own, near, far, pending):
    step = pl.program_id(0)

    @pl.when(step == 0)
    def _():
        pending[...] = jnp.zeros_like(pending)

    batch = rhs.shape[0]
    values = []
    for i in range(batch):
        value = times(inverse[i], rhs[i])
        solved[i] = value
        values.append(value)
    for i in range(batch):
        pending[links[0, step * batch + i]] += times(first[i, 0], values[i])

    @pl.when(step == pl.num_programs(0) - 1)
    def _():
        own[...] = pending[0]
        near[...] = pending[1]
        far[...] = pending[2]


def root_terms_kernel(links, one, two, three, solved, after, pending):
    step = pl.program_id(0)

    @pl.when(step == 0)
    def _():
        pending[...] = jnp.zeros_like(pending)

    batch = solved.shape[0]
    for i in range(batch):
        blocks = jnp.concatenate([one[i, 0], two[i, 0], three[i, 0]], axis=0)
        terms = times(blocks, solved[i])
        for n in range(3):
            slot = links[n + 1, step * batch + i] - 3
            pending[slot] += terms[n * 128 : n * 128 + 128]


def root_operator_kernel(
    lower_inverse, upper_inverse, lower, upper, after, root_operator, forward, backward
):
    count = lower_inverse.shape[0]
    w = lower_inverse.shape[1]
    forward[...] = jnp.zeros_like(forward)
    backward[...] = jnp.zeros_like(backward)
    for r in range(count):
        here = slice(r * w, r * w + w)
        forward[here, here] = lower_inverse[r]
        if r > 0:
            done = slice(0, r * w)
            inner = times(lower[here, done], forward[done, done])
            forward[here, done] = -times(lower_inverse[r], inner)
    for r in reversed(range(count)):
        here = slice(r * w, r * w + w)
        backward[here, here] = upper_inverse[r]
        if r < count - 1:
            done = slice((r + 1) * w, count * w)
            inner = times(upper[here, done], backward[done, done])
            backward[here, done] = -times(upper_inverse[r], inner)
    for r in range(count):
        here = slice(r * w, r * w + w)
        left = as_left(times(backward[here, r * w :], forward[r * w :, :]))
        root_operator[here, :] = left[:w]
        root_operator[count * w + r * w : count * w + r * w + w, :] = left[w:]


def separator_operators_kernel(
    lower_inverse, upper_inverse, lower, upper, after, forward, backward
):
    blocks = jnp.concatenate([upper_inverse[0]] + [lower[0, n] for n in range(3)], axis=0)
    forward[...] = as_left(times(blocks, lower_inverse[0]))
    blocks = jnp.concatenate([upper[0, n] for n in range(3)], axis=1)
    backward[...] = as_left(times(upper_inverse[0], blocks))


def separator_kernel(
    links, core, rhs, operator, own, near, far, root_pending, solved, mine, theirs, sums
):
    right = as_right(rhs[0] - own[...] - near[...] - far[...])
    terms = left_times(operator[...], right)
    solved[...] = terms[:128]
    sums[...] = root_pending[...]
    for n in range(3):
        sums[links[n]] += terms[n * 128 + 128 : n * 128 + 256]
    is_first = core[0] == 0

    @pl.when(is_first)
    def _():
        mine[...] = sums[:, :, :128]
        theirs[...] = sums[:, :, 128:]

    @pl.when(jnp.logical_not(is_first))
    def _():
        mine[...] = sums[:, :, 128:]
        theirs[...] = sums[:, :, :128]


def pieces_kernel(place, mine, other, *pieces):
    position = place[0]
    for j, piece in enumerate(pieces):
        piece[...] = mine[position ^ j] + other[position ^ j]


def root_kernel(place, rhs, operator, own, one, two, three, out, pending):
    count, w = rhs.shape[0], rhs.shape[1]
    position = place[0]
    is_first = place[1] == 0
    for j, piece in enumerate((own, one, two, three)):
        root = position ^ j
        right = rhs[root]
        right = jnp.where(is_first, right[:, :128], right[:, 128:])
        pending[pl.ds(pl.multiple_of(root * 2 * w, 2 * w), 2 * w), :] = as_right(
            right - piece[...]
        )
    out[...] = left_times(operator[...], pending[...]).reshape(count, w, 128)


def separator_back_kernel(links, core, mine, theirs, operator, solved, root_sol, right, out):
    is_first = core[0] == 0

    @pl.when(is_first)
    def _():
        root_sol[:, :, :128] = mine[...]
        root_sol[:, :, 128:] = theirs[...]

    @pl.when(jnp.logical_not(is_first))
    def _():
        root_sol[:, :, :128] = theirs[...]
        root_sol[:, :, 128:] = mine[...]

    for r in range(root_sol.shape[0]):
        right[r] = as_right(root_sol[r])
    linked = jnp.concatenate([right[links[n]] for n in range(3)], axis=0)
    out[0] = solved[...] - left_times(operator[...], linked)


def leaf_operator_kernel(inverse, first, after, operator):
    for i in range(inverse.shape[0]):
        operator[i] = as_left(times(inverse[i], first[i, 0]))


def leaf_root_part_kernel(links, one, two, three, inverse, solved, root_right, part):
    step = pl.program_id(0)
    batch = solved.shape[0]
    rests = []
    for i in range(batch):
        leaf = step * batch + i
        blocks = jnp.concatenate([one[i, 0], two[i, 0], three[i, 0]], axis=1)
        linked = jnp.concatenate([root_right[links[n, leaf] - 3] for n in (1, 2, 3)], axis=0)
        rests.append(solved[i] - left_times(as_left(blocks), linked))
    for i in range(batch):
        part[i] = times(inverse[i], rests[i])


def leaf_final_kernel(links, operator, part, own, near, far, out, seps):
    step = pl.program_id(0)

    @pl.when(step == 0)
    def _():
        seps[0] = as_right(own[0])
        seps[1] = as_right(near[...])
        seps[2] = as_right(far[...])

    batch = part.shape[0]
    for i in range(batch):
        slot = links[0, step * batch + i]
        out[i] = part[i] - left_times(operator[i], seps[slot])


def whole(memory=VMEM):
    return pl.BlockSpec(memory_space=memory)


ANY = pl.BlockSpec(memory_space=pl.ANY)


def limit(megabytes):
    return pltpu.CompilerParams(vmem_limit_bytes=megabytes * 1024 * 1024)


def leafwise(batch, *tail):
    return pl.BlockSpec((batch,) + tail, lambda k: (k,) + (0,) * len(tail))


def link(batch, n, w):
    return pl.BlockSpec((batch, 1, w, w), lambda k: (k, n, 0, 0))


def kept(*shape):
    return pl.BlockSpec(shape, lambda k: (0,) * len(shape))


def per_device(
    leaf_rhs,
    leaf_lower_inverse,
    leaf_upper_inverse,
    leaf_lower,
    leaf_upper,
    leaf_rows,
    separator_right_sides,
    separator_lower_inverse,
    separator_upper_inverse,
    separator_lower_blocks,
    sep_upper,
    sep_rows,
    root_rhs,
    root_lower_inverse,
    root_upper_inverse,
    root_lower,
    root_upper,
):
    peers = lax.axis_size("grid")
    leaves, w, columns = leaf_rhs.shape
    roots = root_rhs.shape[0]
    half = columns // 2
    batch = leaves // 2
    position = lax.axis_index("grid") % 4
    core = lax.axis_index("layer")
    core_ref = core.astype(jnp.int32).reshape(1)
    place = jnp.stack([position, core]).astype(jnp.int32)
    leaf_links = leaf_rows.T
    sep_links = sep_rows.reshape(-1)

    def shifted(x, by):
        return lax.ppermute(x, "grid", [(i, (i + by) % peers) for i in range(peers)])

    def crossed(x, bit):
        return lax.ppermute(x, "grid", [(i, i ^ bit) for i in range(peers)])

    def swapped(x):
        return lax.ppermute(x, "layer", [(0, 1), (1, 0)])

    shape = jax.ShapeDtypeStruct

    leaf_solved, own, near, far = pl.pallas_call(
        forward_leaf_kernel,
        grid=(leaves // batch,),
        in_specs=[
            whole(SMEM),
            leafwise(batch, w, columns),
            leafwise(batch, w, w),
            link(batch, 0, w),
        ],
        out_specs=[leafwise(batch, w, columns)] + [kept(w, columns)] * 3,
        out_shape=[shape((leaves, w, columns), F32)] + [shape((w, columns), F32)] * 3,
        scratch_shapes=[VMEM((3, w, columns), F32)],
        compiler_params=limit(56),
        cost_estimate=cost(4),
        name="leaf_forward",
    )(leaf_links, leaf_rhs, leaf_lower_inverse, leaf_lower)

    near_sum = shifted(near, -1)
    far_sum = shifted(far, -(peers // 2))

    root_pending = pl.pallas_call(
        root_terms_kernel,
        grid=(leaves // batch,),
        in_specs=[
            whole(SMEM),
            link(batch, 1, w),
            link(batch, 2, w),
            link(batch, 3, w),
            leafwise(batch, w, columns),
            ANY,
        ],
        out_specs=kept(roots, w, columns),
        out_shape=shape((roots, w, columns), F32),
        compiler_params=limit(16),
        cost_estimate=cost(3),
        name="root_terms",
    )(leaf_links, leaf_lower, leaf_lower, leaf_lower, leaf_solved, own)

    sep_forward, sep_backward = pl.pallas_call(
        separator_operators_kernel,
        in_specs=[whole()] * 4 + [ANY],
        out_specs=[whole()] * 2,
        out_shape=[shape((8 * w, 2 * w), BF16), shape((2 * w, 6 * w), BF16)],
        compiler_params=limit(16),
        cost_estimate=cost(1),
        name="separator_operators",
    )(
        separator_lower_inverse,
        separator_upper_inverse,
        separator_lower_blocks,
        sep_upper,
        own,
    )

    sep_solved, mine, theirs = pl.pallas_call(
        separator_kernel,
        in_specs=[whole(SMEM), whole(SMEM)] + [whole()] * 6,
        out_specs=[whole()] * 3,
        out_shape=[
            shape((w, columns), F32),
            shape((roots, w, half), F32),
            shape((roots, w, half), F32),
        ],
        scratch_shapes=[VMEM((roots, w, columns), F32)],
        compiler_params=limit(16),
        cost_estimate=cost(2),
        name="separator_forward",
    )(
        sep_links,
        core_ref,
        separator_right_sides,
        sep_forward,
        own,
        near_sum,
        far_sum,
        root_pending,
    )

    other = swapped(theirs)
    pieces = pl.pallas_call(
        pieces_kernel,
        in_specs=[whole(SMEM)] + [whole()] * 2,
        out_specs=[whole()] * 4,
        out_shape=[shape((w, half), F32)] * 4,
        compiler_params=limit(16),
        cost_estimate=cost(0.5),
        name="pieces",
    )(place, mine, other)
    total = pieces[0]
    for j in (1, 2, 3):
        total = total + crossed(pieces[j], j)

    leaf_operator = pl.pallas_call(
        leaf_operator_kernel,
        grid=(leaves // batch,),
        in_specs=[leafwise(batch, w, w), link(batch, 0, w), ANY],
        out_specs=leafwise(batch, 2 * w, 2 * w),
        out_shape=shape((leaves, 2 * w, 2 * w), BF16),
        compiler_params=limit(16),
        cost_estimate=cost(1),
        name="leaf_operators",
    )(leaf_upper_inverse, leaf_upper, total)

    root_operator = pl.pallas_call(
        root_operator_kernel,
        in_specs=[whole()] * 4 + [ANY],
        out_specs=whole(),
        out_shape=shape((2 * roots * w, 2 * roots * w), BF16),
        scratch_shapes=[VMEM((roots * w, roots * w), F32)] * 2,
        compiler_params=limit(16),
        cost_estimate=cost(3),
        name="root_operator",
    )(root_lower_inverse, root_upper_inverse, root_lower, root_upper, total)

    bit = 4
    while bit < peers:
        total = total + crossed(total, bit)
        bit *= 2
    others = [crossed(total, j) for j in (1, 2, 3)]

    solution_half = pl.pallas_call(
        root_kernel,
        in_specs=[whole(SMEM)] + [whole()] * 6,
        out_specs=whole(),
        out_shape=shape((roots, w, half), F32),
        scratch_shapes=[VMEM((2 * roots * w, half), BF16)],
        compiler_params=limit(16),
        cost_estimate=cost(1),
        name="root_solve",
    )(place, root_rhs, root_operator, total, *others)

    other_half = swapped(solution_half)

    root_sol, root_right, separator_solution_rows = pl.pallas_call(
        separator_back_kernel,
        in_specs=[whole(SMEM), whole(SMEM)] + [whole()] * 4,
        out_specs=[whole()] * 3,
        out_shape=[
            shape((roots, w, columns), F32),
            shape((roots, 2 * w, columns), BF16),
            shape((1, w, columns), F32),
        ],
        compiler_params=limit(16),
        cost_estimate=cost(1.5),
        name="separator_backward",
    )(sep_links, core_ref, solution_half, other_half, sep_backward, sep_solved)

    near_rows = shifted(separator_solution_rows[0], 1)
    far_rows = shifted(separator_solution_rows[0], peers // 2)

    leaf_part = pl.pallas_call(
        leaf_root_part_kernel,
        grid=(leaves // batch,),
        in_specs=[
            whole(SMEM),
            link(batch, 1, w),
            link(batch, 2, w),
            link(batch, 3, w),
            leafwise(batch, w, w),
            leafwise(batch, w, columns),
            kept(roots, 2 * w, columns),
        ],
        out_specs=leafwise(batch, w, columns),
        out_shape=shape((leaves, w, columns), F32),
        compiler_params=limit(16),
        cost_estimate=cost(3),
        name="leaf_root_part",
    )(
        leaf_links,
        leaf_upper,
        leaf_upper,
        leaf_upper,
        leaf_upper_inverse,
        leaf_solved,
        root_right,
    )

    leaf_sol = pl.pallas_call(
        leaf_final_kernel,
        grid=(leaves // batch,),
        in_specs=[
            whole(SMEM),
            leafwise(batch, 2 * w, 2 * w),
            leafwise(batch, w, columns),
            kept(1, w, columns),
            kept(w, columns),
            kept(w, columns),
        ],
        out_specs=leafwise(batch, w, columns),
        out_shape=shape((leaves, w, columns), F32),
        scratch_shapes=[VMEM((3, 2 * w, columns), BF16)],
        compiler_params=limit(16),
        cost_estimate=cost(2.3),
        name="leaf_backward",
    )(leaf_links, leaf_operator, leaf_part, separator_solution_rows, near_rows, far_rows)
    return (leaf_sol, separator_solution_rows, root_sol)


def solution(mesh):
    by_device = P(("groups", "grid", "layer"))
    by_group = P("groups")
    return jax.shard_map(
        per_device,
        mesh=mesh,
        in_specs=(by_device,) * 12 + (by_group,) * 5,
        out_specs=(by_device, by_device, by_group),
        check_vma=False,
    )
```

```python
import functools

import jax
import jax.numpy as jnp
from jax import lax
from jax.experimental import pallas as pl
from jax.experimental.pallas import tpu as pltpu
from jax.sharding import PartitionSpec as P

VMEM = pltpu.VMEM
SMEM = pltpu.SMEM
F32 = jnp.float32
BF16 = jnp.bfloat16


def parts_of(x):
    high = x.astype(BF16)
    low = (x - high.astype(F32)).astype(BF16)
    return high, low


def as_left(x):
    high, low = parts_of(x)
    count = x.shape[1] // 128
    pieces = [slice(j * 128, j * 128 + 128) for j in range(count)]
    top = jnp.concatenate([high[:, s] for s in pieces for _ in range(2)], axis=1)
    bottom = jnp.concatenate([low[:, s] for s in pieces for _ in range(2)], axis=1)
    return jnp.concatenate([top, bottom], axis=0)


def as_right(x):
    high, low = parts_of(x)
    count = x.shape[0] // 128
    pieces = [slice(j * 128, j * 128 + 128) for j in range(count)]
    return jnp.concatenate([y[s] for s in pieces for y in (high, low)], axis=0)


def left_times(left, right):
    both = jnp.dot(left, right, preferred_element_type=F32)
    rows = left.shape[0] // 2
    return both[:rows] + both[rows:]


def times(a, b):
    return left_times(as_left(a), as_right(b))


def cost(microseconds):
    return pl.CostEstimate(
        flops=int(microseconds * 1e9),
        bytes_accessed=int(microseconds * 3e6),
        transcendentals=0,
    )


def forward_leaf_kernel(links, rhs, inverse, first, solved, own, near, far, pending):
    step = pl.program_id(0)

    @pl.when(step == 0)
    def _():
        pending[...] = jnp.zeros_like(pending)

    batch = rhs.shape[0]
    values = []
    for i in range(batch):
        value = times(inverse[i], rhs[i])
        solved[i] = value
        values.append(value)
    for i in range(batch):
        pending[links[0, step * batch + i]] += times(first[i, 0], values[i])

    @pl.when(step == pl.num_programs(0) - 1)
    def _():
        own[...] = pending[0]
        near[...] = pending[1]
        far[...] = pending[2]


def root_terms_kernel(links, one, two, three, solved, pending):
    step = pl.program_id(0)

    @pl.when(step == 0)
    def _():
        pending[...] = jnp.zeros_like(pending)

    batch = solved.shape[0]
    for i in range(batch):
        blocks = jnp.concatenate([one[i, 0], two[i, 0], three[i, 0]], axis=0)
        terms = times(blocks, solved[i])
        for n in range(3):
            slot = links[n + 1, step * batch + i] - 3
            pending[slot] += terms[n * 128 : n * 128 + 128]


def root_sweeps_kernel(lower_inverse, upper_inverse, lower, upper, after, forward, backward):
    count = lower_inverse.shape[0]
    w = lower_inverse.shape[1]
    forward[...] = jnp.zeros_like(forward)
    backward[...] = jnp.zeros_like(backward)
    for step in range(count):
        r = step
        here = slice(r * w, r * w + w)
        forward[here, here] = lower_inverse[r]
        if step > 0:
            done = slice(0, r * w)
            inner = times(lower[here, done], forward[done, done])
            forward[here, done] = -times(lower_inverse[r], inner)
        r = count - 1 - step
        here = slice(r * w, r * w + w)
        backward[here, here] = upper_inverse[r]
        if step > 0:
            done = slice((r + 1) * w, count * w)
            inner = times(upper[here, done], backward[done, done])
            backward[here, done] = -times(upper_inverse[r], inner)


def root_operator_kernel(forward, backward, after, root_operator):
    w = 128
    size = forward.shape[0]
    for r in range(0, size, w):
        left = as_left(times(backward[r : r + w, r:], forward[r:, :]))
        root_operator[r : r + w, :] = left[:w]
        root_operator[size + r : size + r + w, :] = left[w:]


def separator_operators_kernel(
    lower_inverse, upper_inverse, lower, upper, after, forward, part, backward
):
    blocks = jnp.concatenate([lower[0, n] for n in range(3)], axis=0)
    forward[...] = as_left(times(blocks, lower_inverse[0]))
    part[...] = as_left(times(upper_inverse[0], lower_inverse[0]))
    blocks = jnp.concatenate([upper[0, n] for n in range(3)], axis=1)
    backward[...] = as_left(times(upper_inverse[0], blocks))


def separator_kernel(
    links, place, rhs, operator, own, near, far, root_pending, right, mine, theirs, sums
):
    right[...] = as_right(rhs[0] - own[...] - near[...] - far[...])
    terms = left_times(operator[...], right[...])
    sums[...] = root_pending[...]
    for n in range(3):
        sums[links[n]] += terms[n * 128 : n * 128 + 128]
    position = place[0]
    is_first = place[1] == 0
    for j in range(4):
        block = sums[position ^ j]
        first, second = block[:, :128], block[:, 128:]
        mine[j] = jnp.where(is_first, first, second)
        theirs[j] = jnp.where(is_first, second, first)


def separator_part_kernel(operator, right, out):
    out[...] = left_times(operator[...], right[...])


def root_kernel(place, rhs, operator, own, one, two, three, out, pending):
    count, w = rhs.shape[0], rhs.shape[1]
    position = place[0]
    is_first = place[1] == 0
    for j, piece in enumerate((own, one, two, three)):
        root = position ^ j
        right = rhs[root]
        right = jnp.where(is_first, right[:, :128], right[:, 128:])
        pending[pl.ds(pl.multiple_of(root * 2 * w, 2 * w), 2 * w), :] = as_right(
            right - piece[...]
        )
    out[...] = left_times(operator[...], pending[...]).reshape(count, w, 128)


def separator_back_kernel(links, core, mine, theirs, operator, part, right, out):
    is_first = core[0] == 0
    for r in range(mine.shape[0]):
        one, other = as_right(mine[r]), as_right(theirs[r])
        right[r, :, :128] = jnp.where(is_first, one, other)
        right[r, :, 128:] = jnp.where(is_first, other, one)
    linked = jnp.concatenate([right[links[n]] for n in range(3)], axis=0)
    out[...] = part[...] - left_times(operator[...], linked)


def leaf_operator_kernel(inverse, first, after, operator):
    for i in range(inverse.shape[0]):
        operator[i] = as_left(times(inverse[i], first[i, 0]))


def leaf_root_part_kernel(
    links,
    core,
    one,
    two,
    three,
    inverse,
    solved,
    root_right,
    mine,
    theirs,
    sep_sol,
    part,
    root_sol,
    sep_rows,
):
    step = pl.program_id(0)

    @pl.when(step == 0)
    def _():
        is_first = core[0] == 0
        sep_rows[0] = sep_sol[...]
        root_sol[:, :, :128] = jnp.where(is_first, mine[...], theirs[...])
        root_sol[:, :, 128:] = jnp.where(is_first, theirs[...], mine[...])

    batch = solved.shape[0]
    rests = []
    for i in range(batch):
        leaf = step * batch + i
        blocks = jnp.concatenate([one[i, 0], two[i, 0], three[i, 0]], axis=1)
        linked = jnp.concatenate([root_right[links[n, leaf] - 3] for n in (1, 2, 3)], axis=0)
        rests.append(solved[i] - left_times(as_left(blocks), linked))
    for i in range(batch):
        part[i] = times(inverse[i], rests[i])


def leaf_final_kernel(links, operator, part, own, near, far, out, seps, ready, sems):
    seps[0] = as_right(own[...])
    seps[1] = as_right(near[...])
    seps[2] = as_right(far[...])
    count = part.shape[0]
    copies = []
    for i in range(count):
        ready[i] = part[i] - left_times(operator[i], seps[links[0, i]])
        if i % 2 == 1:
            pair = pl.ds(i - 1, 2)
            copy = pltpu.make_async_copy(ready.at[pair], out.at[pair], sems.at[i // 2])
            copy.start()
            copies.append(copy)
    for copy in copies:
        copy.wait()


def whole(memory=VMEM):
    return pl.BlockSpec(memory_space=memory)


ANY = pl.BlockSpec(memory_space=pl.ANY)


def limit(megabytes):
    return pltpu.CompilerParams(vmem_limit_bytes=megabytes * 1024 * 1024)


def leafwise(batch, *tail):
    return pl.BlockSpec((batch,) + tail, lambda k: (k,) + (0,) * len(tail))


def link(batch, n, w):
    return pl.BlockSpec((batch, 1, w, w), lambda k: (k, n, 0, 0))


def kept(*shape):
    return pl.BlockSpec(shape, lambda k: (0,) * len(shape))


def per_device(
    leaf_rhs,
    leaf_lower_inverse,
    leaf_upper_inverse,
    leaf_lower,
    leaf_upper,
    leaf_rows,
    separator_right_sides,
    separator_lower_inverse,
    separator_upper_inverse,
    separator_lower_blocks,
    sep_upper,
    sep_rows,
    root_rhs,
    root_lower_inverse,
    root_upper_inverse,
    root_lower,
    root_upper,
):
    peers = lax.axis_size("grid")
    leaves, w, columns = leaf_rhs.shape
    roots = root_rhs.shape[0]
    half = columns // 2
    batch = leaves // 2
    position = lax.axis_index("grid") % 4
    core = lax.axis_index("layer")
    core_ref = core.astype(jnp.int32).reshape(1)
    place = jnp.stack([position, core]).astype(jnp.int32)
    leaf_links = leaf_rows.T
    sep_links = sep_rows.reshape(-1)

    def shifted(x, by):
        return lax.ppermute(x, "grid", [(i, (i + by) % peers) for i in range(peers)])

    def crossed(x, bit):
        return lax.ppermute(x, "grid", [(i, i ^ bit) for i in range(peers)])

    def swapped(x):
        return lax.ppermute(x, "layer", [(0, 1), (1, 0)])

    shape = jax.ShapeDtypeStruct

    leaf_solved, own, near, far = pl.pallas_call(
        forward_leaf_kernel,
        grid=(leaves // batch,),
        in_specs=[
            whole(SMEM),
            leafwise(batch, w, columns),
            leafwise(batch, w, w),
            link(batch, 0, w),
        ],
        out_specs=[leafwise(batch, w, columns)] + [kept(w, columns)] * 3,
        out_shape=[shape((leaves, w, columns), F32)] + [shape((w, columns), F32)] * 3,
        scratch_shapes=[VMEM((3, w, columns), F32)],
        compiler_params=limit(56),
        cost_estimate=cost(4),
        name="leaf_forward",
    )(leaf_links, leaf_rhs, leaf_lower_inverse, leaf_lower)

    far_sum = shifted(far, -(peers // 2))
    near_sum = shifted(near, -1)

    root_pending = pl.pallas_call(
        root_terms_kernel,
        grid=(leaves // batch,),
        in_specs=[
            whole(SMEM),
            link(batch, 1, w),
            link(batch, 2, w),
            link(batch, 3, w),
            leafwise(batch, w, columns),
        ],
        out_specs=kept(roots, w, columns),
        out_shape=shape((roots, w, columns), F32),
        compiler_params=limit(16),
        cost_estimate=cost(3),
        name="root_terms",
    )(leaf_links, leaf_lower, leaf_lower, leaf_lower, leaf_solved)

    sep_forward, sep_part, sep_backward = pl.pallas_call(
        separator_operators_kernel,
        in_specs=[whole()] * 4 + [ANY],
        out_specs=[whole()] * 3,
        out_shape=[
            shape((6 * w, 2 * w), BF16),
            shape((2 * w, 2 * w), BF16),
            shape((2 * w, 6 * w), BF16),
        ],
        compiler_params=limit(16),
        cost_estimate=cost(1),
        name="separator_operators",
    )(
        separator_lower_inverse,
        separator_upper_inverse,
        separator_lower_blocks,
        sep_upper,
        leaf_solved,
    )

    sep_right, mine, theirs = pl.pallas_call(
        separator_kernel,
        in_specs=[whole(SMEM), whole(SMEM)] + [whole()] * 6,
        out_specs=[whole()] * 3,
        out_shape=[
            shape((2 * w, columns), BF16),
            shape((roots, w, half), F32),
            shape((roots, w, half), F32),
        ],
        scratch_shapes=[VMEM((roots, w, columns), F32)],
        compiler_params=limit(16),
        cost_estimate=cost(2),
        name="separator_forward",
    )(
        sep_links,
        place,
        separator_right_sides,
        sep_forward,
        own,
        near_sum,
        far_sum,
        root_pending,
    )

    other = swapped(theirs)
    sep_solved = pl.pallas_call(
        separator_part_kernel,
        in_specs=[whole()] * 2,
        out_specs=whole(),
        out_shape=shape((w, columns), F32),
        compiler_params=limit(16),
        cost_estimate=cost(0.4),
        name="separator_part",
    )(sep_part, sep_right)
    pieces = [mine[j] + other[j] for j in range(4)]
    forward, backward = pl.pallas_call(
        root_sweeps_kernel,
        in_specs=[whole()] * 4 + [ANY],
        out_specs=[whole()] * 2,
        out_shape=[shape((roots * w, roots * w), F32)] * 2,
        compiler_params=limit(16),
        cost_estimate=cost(2.3),
        name="root_sweeps",
    )(root_lower_inverse, root_upper_inverse, root_lower, root_upper, pieces[1])
    arrived = [crossed(pieces[j], j) for j in (1, 2, 3)]
    arrived, forward, backward = lax.optimization_barrier((arrived, forward, backward))
    total = pieces[0] + arrived[0] + arrived[1] + arrived[2]

    root_operator = pl.pallas_call(
        root_operator_kernel,
        in_specs=[whole()] * 2 + [ANY],
        out_specs=whole(),
        out_shape=shape((2 * roots * w, 2 * roots * w), BF16),
        compiler_params=limit(16),
        cost_estimate=cost(1),
        name="root_operator",
    )(forward, backward, total)

    bit = 4
    while bit < peers:
        arrived = crossed(total, bit)
        if bit == 4:
            arrived, root_operator = lax.optimization_barrier((arrived, root_operator))
        total = total + arrived
        bit *= 2
    others = [crossed(total, j) for j in (1, 2, 3)]

    solution_half = pl.pallas_call(
        root_kernel,
        in_specs=[whole(SMEM)] + [whole()] * 6,
        out_specs=whole(),
        out_shape=shape((roots, w, half), F32),
        scratch_shapes=[VMEM((2 * roots * w, half), BF16)],
        compiler_params=limit(16),
        cost_estimate=cost(1),
        name="root_solve",
    )(place, root_rhs, root_operator, total, *others)

    other_half = swapped(solution_half)

    root_right, sep_sol = pl.pallas_call(
        separator_back_kernel,
        in_specs=[whole(SMEM), whole(SMEM)] + [whole()] * 4,
        out_specs=[whole()] * 2,
        out_shape=[shape((roots, 2 * w, columns), BF16), shape((w, columns), F32)],
        compiler_params=limit(16),
        cost_estimate=cost(1.5),
        name="separator_backward",
    )(sep_links, core_ref, solution_half, other_half, sep_backward, sep_solved)

    far_rows = shifted(sep_sol, peers // 2)
    near_rows = shifted(sep_sol, 1)

    leaf_operator = pl.pallas_call(
        leaf_operator_kernel,
        grid=(leaves // batch,),
        in_specs=[leafwise(batch, w, w), link(batch, 0, w), ANY],
        out_specs=leafwise(batch, 2 * w, 2 * w),
        out_shape=shape((leaves, 2 * w, 2 * w), BF16),
        compiler_params=limit(16),
        cost_estimate=cost(1),
        name="leaf_operators",
    )(leaf_upper_inverse, leaf_upper, sep_sol)

    leaf_part, root_sol, separator_solution_rows = pl.pallas_call(
        leaf_root_part_kernel,
        grid=(leaves // batch,),
        in_specs=[
            whole(SMEM),
            whole(SMEM),
            link(batch, 1, w),
            link(batch, 2, w),
            link(batch, 3, w),
            leafwise(batch, w, w),
            leafwise(batch, w, columns),
            kept(roots, 2 * w, columns),
            kept(roots, w, half),
            kept(roots, w, half),
            kept(w, columns),
        ],
        out_specs=[
            leafwise(batch, w, columns),
            kept(roots, w, columns),
            kept(1, w, columns),
        ],
        out_shape=[
            shape((leaves, w, columns), F32),
            shape((roots, w, columns), F32),
            shape((1, w, columns), F32),
        ],
        compiler_params=limit(16),
        cost_estimate=cost(3),
        name="leaf_root_part",
    )(
        leaf_links,
        core_ref,
        leaf_upper,
        leaf_upper,
        leaf_upper,
        leaf_upper_inverse,
        leaf_solved,
        root_right,
        solution_half,
        other_half,
        sep_sol,
    )

    leaf_sol = pl.pallas_call(
        leaf_final_kernel,
        in_specs=[whole(SMEM)] + [whole()] * 5,
        out_specs=ANY,
        out_shape=shape((leaves, w, columns), F32),
        scratch_shapes=[
            VMEM((3, 2 * w, columns), BF16),
            VMEM((leaves, w, columns), F32),
            pltpu.SemaphoreType.DMA((leaves // 2,)),
        ],
        compiler_params=limit(16),
        cost_estimate=cost(2),
        name="leaf_backward",
    )(leaf_links, leaf_operator, leaf_part, sep_sol, near_rows, far_rows)
    return (leaf_sol, separator_solution_rows, root_sol)


def solution(mesh):
    by_device = P(("groups", "grid", "layer"))
    by_group = P("groups")
    return jax.shard_map(
        per_device,
        mesh=mesh,
        in_specs=(by_device,) * 12 + (by_group,) * 5,
        out_specs=(by_device, by_device, by_group),
        check_vma=False,
    )
```

```python
import functools

import jax
import jax.numpy as jnp
from jax import lax
from jax.experimental import pallas as pl
from jax.experimental.pallas import tpu as pltpu
from jax.sharding import PartitionSpec as P

VMEM = pltpu.VMEM
SMEM = pltpu.SMEM
F32 = jnp.float32
BF16 = jnp.bfloat16


def parts_of(x):
    high = x.astype(BF16)
    low = (x - high.astype(F32)).astype(BF16)
    return high, low


def as_left(x):
    high, low = parts_of(x)
    count = x.shape[1] // 128
    pieces = [slice(j * 128, j * 128 + 128) for j in range(count)]
    top = jnp.concatenate([high[:, s] for s in pieces for _ in range(2)], axis=1)
    bottom = jnp.concatenate([low[:, s] for s in pieces for _ in range(2)], axis=1)
    return jnp.concatenate([top, bottom], axis=0)


def as_right(x):
    high, low = parts_of(x)
    count = x.shape[0] // 128
    pieces = [slice(j * 128, j * 128 + 128) for j in range(count)]
    return jnp.concatenate([y[s] for s in pieces for y in (high, low)], axis=0)


def left_times(left, right):
    both = jnp.dot(left, right, preferred_element_type=F32)
    rows = left.shape[0] // 2
    return both[:rows] + both[rows:]


def times(a, b):
    return left_times(as_left(a), as_right(b))


def cost(microseconds):
    return pl.CostEstimate(
        flops=int(microseconds * 1e9),
        bytes_accessed=int(microseconds * 3e6),
        transcendentals=0,
    )


def forward_leaf_kernel(links, rhs, inverse, first, solved, own, far, near, pending):
    step = pl.program_id(0)

    @pl.when(step == 0)
    def _():
        pending[...] = jnp.zeros_like(pending)

    batch = rhs.shape[0]
    values = []
    for i in range(batch):
        value = times(inverse[i], rhs[i])
        solved[i] = value
        values.append(value)
    for i in range(batch):
        pending[links[0, step * batch + i]] += times(first[i, 0], values[i])

    @pl.when(step == pl.num_programs(0) - 1)
    def _():
        own[...] = pending[0]
        near[...] = pending[1]
        far[...] = pending[2]


def root_terms_kernel(links, one, two, three, solved, pending):
    step = pl.program_id(0)

    @pl.when(step == 0)
    def _():
        pending[...] = jnp.zeros_like(pending)

    batch = solved.shape[0]
    for i in range(batch):
        blocks = jnp.concatenate([one[i, 0], two[i, 0], three[i, 0]], axis=0)
        terms = times(blocks, solved[i])
        for n in range(3):
            slot = links[n + 1, step * batch + i] - 3
            pending[slot] += terms[n * 128 : n * 128 + 128]


def root_sweeps_kernel(lower_inverse, upper_inverse, lower, upper, after, forward, backward):
    count = lower_inverse.shape[0]
    w = lower_inverse.shape[1]
    forward[...] = jnp.zeros_like(forward)
    backward[...] = jnp.zeros_like(backward)
    for step in range(count):
        r = step
        here = slice(r * w, r * w + w)
        forward[here, here] = lower_inverse[r]
        if step > 0:
            done = slice(0, r * w)
            inner = times(lower[here, done], forward[done, done])
            forward[here, done] = -times(lower_inverse[r], inner)
        r = count - 1 - step
        here = slice(r * w, r * w + w)
        backward[here, here] = upper_inverse[r]
        if step > 0:
            done = slice((r + 1) * w, count * w)
            inner = times(upper[here, done], backward[done, done])
            backward[here, done] = -times(upper_inverse[r], inner)


def root_operator_kernel(forward, backward, after, root_operator):
    w = 128
    size = forward.shape[0]
    for r in range(0, size, w):
        left = as_left(times(backward[r : r + w, r:], forward[r:, :]))
        root_operator[r : r + w, :] = left[:w]
        root_operator[size + r : size + r + w, :] = left[w:]


def separator_operators_kernel(
    lower_inverse, upper_inverse, lower, upper, after, forward, part, backward
):
    blocks = jnp.concatenate([lower[0, n] for n in range(3)], axis=0)
    forward[...] = as_left(times(blocks, lower_inverse[0]))
    part[...] = as_left(times(upper_inverse[0], lower_inverse[0]))
    blocks = jnp.concatenate([upper[0, n] for n in range(3)], axis=1)
    backward[...] = as_left(times(upper_inverse[0], blocks))


def separator_kernel(
    links, place, rhs, operator, own, far, near, root_pending, right, mine, theirs, sums
):
    right[...] = as_right(rhs[0] - own[...] - near[...] - far[...])
    terms = left_times(operator[...], right[...])
    sums[...] = root_pending[...]
    for n in range(3):
        sums[links[n]] += terms[n * 128 : n * 128 + 128]
    position = place[0]
    is_first = place[1] == 0
    for j in range(4):
        block = sums[position ^ j]
        first, second = block[:, :128], block[:, 128:]
        mine[j] = jnp.where(is_first, first, second)
        theirs[j] = jnp.where(is_first, second, first)


def separator_part_kernel(operator, right, out):
    out[...] = left_times(operator[...], right[...])


def root_kernel(place, rhs, operator, own, one, two, three, out, pending):
    count, w = rhs.shape[0], rhs.shape[1]
    position = place[0]
    is_first = place[1] == 0
    for j, piece in enumerate((own, one, two, three)):
        root = position ^ j
        right = rhs[root]
        right = jnp.where(is_first, right[:, :128], right[:, 128:])
        pending[pl.ds(pl.multiple_of(root * 2 * w, 2 * w), 2 * w), :] = as_right(
            right - piece[...]
        )
    out[...] = left_times(operator[...], pending[...]).reshape(count, w, 128)


def separator_back_kernel(links, core, mine, theirs, operator, part, right, out):
    is_first = core[0] == 0
    for r in range(mine.shape[0]):
        one, other = as_right(mine[r]), as_right(theirs[r])
        right[r, :, :128] = jnp.where(is_first, one, other)
        right[r, :, 128:] = jnp.where(is_first, other, one)
    linked = jnp.concatenate([right[links[n]] for n in range(3)], axis=0)
    out[...] = part[...] - left_times(operator[...], linked)


def leaf_operator_kernel(inverse, first, after, operator):
    for i in range(inverse.shape[0]):
        operator[i] = as_left(times(inverse[i], first[i, 0]))


def leaf_root_part_kernel(
    links,
    core,
    one,
    two,
    three,
    inverse,
    solved,
    root_right,
    mine,
    theirs,
    sep_sol,
    part,
    root_sol,
    sep_rows,
):
    step = pl.program_id(0)

    @pl.when(step == 0)
    def _():
        is_first = core[0] == 0
        sep_rows[0] = sep_sol[...]
        root_sol[:, :, :128] = jnp.where(is_first, mine[...], theirs[...])
        root_sol[:, :, 128:] = jnp.where(is_first, theirs[...], mine[...])

    batch = solved.shape[0]
    rests = []
    for i in range(batch):
        leaf = step * batch + i
        blocks = jnp.concatenate([one[i, 0], two[i, 0], three[i, 0]], axis=1)
        linked = jnp.concatenate([root_right[links[n, leaf] - 3] for n in (1, 2, 3)], axis=0)
        rests.append(solved[i] - left_times(as_left(blocks), linked))
    for i in range(batch):
        part[i] = times(inverse[i], rests[i])


def leaf_final_kernel(links, operator, part, own, near, far, out, seps, ready, sems):
    seps[0] = as_right(own[...])
    seps[1] = as_right(near[...])
    seps[2] = as_right(far[...])
    count = part.shape[0]
    copies = []
    for i in range(count):
        ready[i] = part[i] - left_times(operator[i], seps[links[0, i]])
        if i % 2 == 1:
            pair = pl.ds(i - 1, 2)
            copy = pltpu.make_async_copy(ready.at[pair], out.at[pair], sems.at[i // 2])
            copy.start()
            copies.append(copy)
    for copy in copies:
        copy.wait()


def whole(memory=VMEM):
    return pl.BlockSpec(memory_space=memory)


ANY = pl.BlockSpec(memory_space=pl.ANY)


def limit(megabytes):
    return pltpu.CompilerParams(vmem_limit_bytes=megabytes * 1024 * 1024)


def leafwise(batch, *tail):
    return pl.BlockSpec((batch,) + tail, lambda k: (k,) + (0,) * len(tail))


def link(batch, n, w):
    return pl.BlockSpec((batch, 1, w, w), lambda k: (k, n, 0, 0))


def kept(*shape):
    return pl.BlockSpec(shape, lambda k: (0,) * len(shape))


def per_device(
    leaf_rhs,
    leaf_lower_inverse,
    leaf_upper_inverse,
    leaf_lower,
    leaf_upper,
    leaf_rows,
    separator_right_sides,
    separator_lower_inverse,
    separator_upper_inverse,
    separator_lower_blocks,
    sep_upper,
    sep_rows,
    root_rhs,
    root_lower_inverse,
    root_upper_inverse,
    root_lower,
    root_upper,
):
    peers = lax.axis_size("grid")
    leaves, w, columns = leaf_rhs.shape
    roots = root_rhs.shape[0]
    half = columns // 2
    batch = leaves // 2
    position = lax.axis_index("grid") % 4
    core = lax.axis_index("layer")
    core_ref = core.astype(jnp.int32).reshape(1)
    place = jnp.stack([position, core]).astype(jnp.int32)
    leaf_links = leaf_rows.T
    sep_links = sep_rows.reshape(-1)

    def shifted(x, by):
        return lax.ppermute(x, "grid", [(i, (i + by) % peers) for i in range(peers)])

    def crossed(x, bit):
        return lax.ppermute(x, "grid", [(i, i ^ bit) for i in range(peers)])

    def swapped(x):
        return lax.ppermute(x, "layer", [(0, 1), (1, 0)])

    shape = jax.ShapeDtypeStruct

    leaf_solved, own, far, near = pl.pallas_call(
        forward_leaf_kernel,
        grid=(leaves // batch,),
        in_specs=[
            whole(SMEM),
            leafwise(batch, w, columns),
            leafwise(batch, w, w),
            link(batch, 0, w),
        ],
        out_specs=[leafwise(batch, w, columns)] + [kept(w, columns)] * 3,
        out_shape=[shape((leaves, w, columns), F32)] + [shape((w, columns), F32)] * 3,
        scratch_shapes=[VMEM((3, w, columns), F32)],
        compiler_params=limit(56),
        cost_estimate=cost(4),
        name="leaf_forward",
    )(leaf_links, leaf_rhs, leaf_lower_inverse, leaf_lower)

    far_sum = shifted(far, -(peers // 2))
    near_sum = shifted(near, -1)

    root_pending = pl.pallas_call(
        root_terms_kernel,
        grid=(leaves // batch,),
        in_specs=[
            whole(SMEM),
            link(batch, 1, w),
            link(batch, 2, w),
            link(batch, 3, w),
            leafwise(batch, w, columns),
        ],
        out_specs=kept(roots, w, columns),
        out_shape=shape((roots, w, columns), F32),
        compiler_params=limit(16),
        cost_estimate=cost(3),
        name="root_terms",
    )(leaf_links, leaf_lower, leaf_lower, leaf_lower, leaf_solved)

    sep_forward, sep_part, sep_backward = pl.pallas_call(
        separator_operators_kernel,
        in_specs=[whole()] * 4 + [ANY],
        out_specs=[whole()] * 3,
        out_shape=[
            shape((6 * w, 2 * w), BF16),
            shape((2 * w, 2 * w), BF16),
            shape((2 * w, 6 * w), BF16),
        ],
        compiler_params=limit(16),
        cost_estimate=cost(1),
        name="separator_operators",
    )(
        separator_lower_inverse,
        separator_upper_inverse,
        separator_lower_blocks,
        sep_upper,
        leaf_solved,
    )

    sep_right, mine, theirs = pl.pallas_call(
        separator_kernel,
        in_specs=[whole(SMEM), whole(SMEM)] + [whole()] * 6,
        out_specs=[whole()] * 3,
        out_shape=[
            shape((2 * w, columns), BF16),
            shape((roots, w, half), F32),
            shape((roots, w, half), F32),
        ],
        scratch_shapes=[VMEM((roots, w, columns), F32)],
        compiler_params=limit(16),
        cost_estimate=cost(2),
        name="separator_forward",
    )(
        sep_links,
        place,
        separator_right_sides,
        sep_forward,
        own,
        far_sum,
        near_sum,
        root_pending,
    )

    other = swapped(theirs)
    sep_solved = pl.pallas_call(
        separator_part_kernel,
        in_specs=[whole()] * 2,
        out_specs=whole(),
        out_shape=shape((w, columns), F32),
        compiler_params=limit(16),
        cost_estimate=cost(0.4),
        name="separator_part",
    )(sep_part, sep_right)
    pieces = [mine[j] + other[j] for j in range(4)]
    forward, backward = pl.pallas_call(
        root_sweeps_kernel,
        in_specs=[whole()] * 4 + [ANY],
        out_specs=[whole()] * 2,
        out_shape=[shape((roots * w, roots * w), F32)] * 2,
        compiler_params=limit(16),
        cost_estimate=cost(2.3),
        name="root_sweeps",
    )(root_lower_inverse, root_upper_inverse, root_lower, root_upper, pieces[1])
    arrived = [crossed(pieces[j], j) for j in (1, 2, 3)]
    arrived, forward, backward = lax.optimization_barrier((arrived, forward, backward))
    total = pieces[0] + arrived[0] + arrived[1] + arrived[2]

    root_operator = pl.pallas_call(
        root_operator_kernel,
        in_specs=[whole()] * 2 + [ANY],
        out_specs=whole(),
        out_shape=shape((2 * roots * w, 2 * roots * w), BF16),
        compiler_params=limit(16),
        cost_estimate=cost(1),
        name="root_operator",
    )(forward, backward, total)

    bit = 4
    while bit < peers:
        arrived = crossed(total, bit)
        if bit == 4:
            arrived, root_operator = lax.optimization_barrier((arrived, root_operator))
        total = total + arrived
        bit *= 2
    others = [crossed(total, j) for j in (1, 2, 3)]

    solution_half = pl.pallas_call(
        root_kernel,
        in_specs=[whole(SMEM)] + [whole()] * 6,
        out_specs=whole(),
        out_shape=shape((roots, w, half), F32),
        scratch_shapes=[VMEM((2 * roots * w, half), BF16)],
        compiler_params=limit(16),
        cost_estimate=cost(1),
        name="root_solve",
    )(place, root_rhs, root_operator, total, *others)

    other_half = swapped(solution_half)

    root_right, sep_sol = pl.pallas_call(
        separator_back_kernel,
        in_specs=[whole(SMEM), whole(SMEM)] + [whole()] * 4,
        out_specs=[whole()] * 2,
        out_shape=[shape((roots, 2 * w, columns), BF16), shape((w, columns), F32)],
        compiler_params=limit(16),
        cost_estimate=cost(1.5),
        name="separator_backward",
    )(sep_links, core_ref, solution_half, other_half, sep_backward, sep_solved)

    far_rows = shifted(sep_sol, peers // 2)
    near_rows = shifted(sep_sol, 1)

    leaf_operator = pl.pallas_call(
        leaf_operator_kernel,
        grid=(leaves // batch,),
        in_specs=[leafwise(batch, w, w), link(batch, 0, w), ANY],
        out_specs=leafwise(batch, 2 * w, 2 * w),
        out_shape=shape((leaves, 2 * w, 2 * w), BF16),
        compiler_params=limit(16),
        cost_estimate=cost(1),
        name="leaf_operators",
    )(leaf_upper_inverse, leaf_upper, sep_sol)

    leaf_part, root_sol, separator_solution_rows = pl.pallas_call(
        leaf_root_part_kernel,
        grid=(leaves // batch,),
        in_specs=[
            whole(SMEM),
            whole(SMEM),
            link(batch, 1, w),
            link(batch, 2, w),
            link(batch, 3, w),
            leafwise(batch, w, w),
            leafwise(batch, w, columns),
            kept(roots, 2 * w, columns),
            kept(roots, w, half),
            kept(roots, w, half),
            kept(w, columns),
        ],
        out_specs=[
            leafwise(batch, w, columns),
            kept(roots, w, columns),
            kept(1, w, columns),
        ],
        out_shape=[
            shape((leaves, w, columns), F32),
            shape((roots, w, columns), F32),
            shape((1, w, columns), F32),
        ],
        compiler_params=limit(16),
        cost_estimate=cost(3),
        name="leaf_root_part",
    )(
        leaf_links,
        core_ref,
        leaf_upper,
        leaf_upper,
        leaf_upper,
        leaf_upper_inverse,
        leaf_solved,
        root_right,
        solution_half,
        other_half,
        sep_sol,
    )

    leaf_sol = pl.pallas_call(
        leaf_final_kernel,
        in_specs=[whole(SMEM)] + [whole()] * 5,
        out_specs=ANY,
        out_shape=shape((leaves, w, columns), F32),
        scratch_shapes=[
            VMEM((3, 2 * w, columns), BF16),
            VMEM((leaves, w, columns), F32),
            pltpu.SemaphoreType.DMA((leaves // 2,)),
        ],
        compiler_params=limit(16),
        cost_estimate=cost(2),
        name="leaf_backward",
    )(leaf_links, leaf_operator, leaf_part, sep_sol, near_rows, far_rows)
    return (leaf_sol, separator_solution_rows, root_sol)


def solution(mesh):
    by_device = P(("groups", "grid", "layer"))
    by_group = P("groups")
    return jax.shard_map(
        per_device,
        mesh=mesh,
        in_specs=(by_device,) * 12 + (by_group,) * 5,
        out_specs=(by_device, by_device, by_group),
        check_vma=False,
    )
```

```python
import functools

import jax
import jax.numpy as jnp
from jax import lax
from jax.experimental import pallas as pl
from jax.experimental.pallas import tpu as pltpu
from jax.sharding import PartitionSpec as P

VMEM = pltpu.VMEM
SMEM = pltpu.SMEM
F32 = jnp.float32
BF16 = jnp.bfloat16


def parts_of(x):
    high = x.astype(BF16)
    low = (x - high.astype(F32)).astype(BF16)
    return high, low


def as_left(x):
    high, low = parts_of(x)
    count = x.shape[1] // 128
    pieces = [slice(j * 128, j * 128 + 128) for j in range(count)]
    top = jnp.concatenate([high[:, s] for s in pieces for _ in range(2)], axis=1)
    bottom = jnp.concatenate([low[:, s] for s in pieces for _ in range(2)], axis=1)
    return jnp.concatenate([top, bottom], axis=0)


def as_right(x):
    high, low = parts_of(x)
    count = x.shape[0] // 128
    pieces = [slice(j * 128, j * 128 + 128) for j in range(count)]
    return jnp.concatenate([y[s] for s in pieces for y in (high, low)], axis=0)


def left_times(left, right):
    both = jnp.dot(left, right, preferred_element_type=F32)
    rows = left.shape[0] // 2
    return both[:rows] + both[rows:]


def times(a, b):
    return left_times(as_left(a), as_right(b))


def halves(is_first, mine, other):
    return jnp.where(is_first, mine, other), jnp.where(is_first, other, mine)


def cost(microseconds):
    return pl.CostEstimate(
        flops=int(microseconds * 1e9),
        bytes_accessed=int(microseconds * 3e6),
        transcendentals=0,
    )


def forward_leaf_kernel(links, rhs, inverse, first, solved, own, far, near, pending):
    step = pl.program_id(0)

    @pl.when(step == 0)
    def _():
        pending[...] = jnp.zeros_like(pending)

    batch = rhs.shape[0]
    values = []
    for i in range(batch):
        value = times(inverse[i], rhs[i])
        solved[i] = value
        values.append(value)
    for i in range(batch):
        pending[links[0, step * batch + i]] += times(first[i, 0], values[i])

    @pl.when(step == pl.num_programs(0) - 1)
    def _():
        own[...] = pending[0]
        near[...] = pending[1]
        far[...] = pending[2]


def root_terms_kernel(links, one, two, three, solved, pending):
    step = pl.program_id(0)

    @pl.when(step == 0)
    def _():
        pending[...] = jnp.zeros_like(pending)

    batch = solved.shape[0]
    for i in range(batch):
        blocks = jnp.concatenate([one[i, 0], two[i, 0], three[i, 0]], axis=0)
        terms = times(blocks, solved[i])
        for n in range(3):
            slot = links[n + 1, step * batch + i] - 3
            pending[slot] += terms[n * 128 : n * 128 + 128]


def root_sweeps_kernel(lower_inverse, upper_inverse, lower, upper, after, forward, backward):
    count = lower_inverse.shape[0]
    w = lower_inverse.shape[1]
    forward[...] = jnp.zeros_like(forward)
    backward[...] = jnp.zeros_like(backward)
    for step in range(count):
        r = step
        here = slice(r * w, r * w + w)
        forward[here, here] = lower_inverse[r]
        if step > 0:
            done = slice(0, r * w)
            inner = times(lower[here, done], forward[done, done])
            forward[here, done] = -times(lower_inverse[r], inner)
        r = count - 1 - step
        here = slice(r * w, r * w + w)
        backward[here, here] = upper_inverse[r]
        if step > 0:
            done = slice((r + 1) * w, count * w)
            inner = times(upper[here, done], backward[done, done])
            backward[here, done] = -times(upper_inverse[r], inner)


def root_operator_kernel(forward, backward, after, root_operator):
    w = 128
    size = forward.shape[0]
    for r in range(0, size, w):
        left = as_left(times(backward[r : r + w, r:], forward[r:, :]))
        root_operator[r : r + w, :] = left[:w]
        root_operator[size + r : size + r + w, :] = left[w:]


def separator_operator_kernel(lower_inverse, lower, after, forward):
    blocks = jnp.concatenate([lower[0, n] for n in range(3)], axis=0)
    forward[...] = as_left(times(blocks, lower_inverse[0]))


def separator_kernel(
    links, place, rhs, operator, own, far, near, root_pending, right, mine, theirs, sums
):
    right[...] = as_right(rhs[0] - own[...] - near[...] - far[...])
    terms = left_times(operator[...], right[...])
    sums[...] = root_pending[...]
    for n in range(3):
        sums[links[n]] += terms[n * 128 : n * 128 + 128]
    position = place[0]
    is_first = place[1] == 0
    for j in range(4):
        block = sums[position ^ j]
        first, second = block[:, :128], block[:, 128:]
        mine[j] = jnp.where(is_first, first, second)
        theirs[j] = jnp.where(is_first, second, first)


def separator_part_kernel(
    links, place, lower_inverse, upper_inverse, upper, right, mine, pack
):
    blocks = jnp.concatenate([upper[0, n] for n in range(3)], axis=1)
    back = times(upper_inverse[0], blocks)
    last = pack.shape[0] - 1
    pack[...] = jnp.zeros_like(pack)
    for n in range(3):
        pack[links[n]] = back[:, n * 128 : n * 128 + 128]
    operator = as_left(times(upper_inverse[0], lower_inverse[0]))
    part = left_times(operator, right[...])
    mine[...], pack[last] = halves(place[1] == 0, part[:, :128], part[:, 128:])


def separator_factors_kernel(pack, other, backward):
    for i, blocks in enumerate((pack, other)):
        backward[i] = as_left(
            jnp.concatenate([blocks[r] for r in range(blocks.shape[0] - 1)], axis=1)
        )


def root_kernel(
    place,
    rhs,
    operator,
    three,
    two,
    one,
    own,
    backward,
    part,
    other_pack,
    out,
    sep_own,
    sep_other,
    pending,
    right,
):
    count, w = rhs.shape[0], rhs.shape[1]
    position = place[0]
    is_first = place[1] == 0
    for j, piece in enumerate((own, one, two, three)):
        root = position ^ j
        side = rhs[root]
        side = jnp.where(is_first, side[:, :128], side[:, 128:])
        pending[pl.ds(pl.multiple_of(root * 2 * w, 2 * w), 2 * w), :] = as_right(
            side - piece[...]
        )
    solution = left_times(operator[...], pending[...])
    for r in range(count):
        out[r] = solution[r * w : r * w + w]
    right[...] = as_right(solution)
    sep_own[...] = part[...] - left_times(backward[0], right[...])
    sep_other[...] = other_pack[count] - left_times(backward[1], right[...])
    out[count] = sep_other[...]


def leaf_operator_kernel(inverse, first, after, operator):
    for i in range(inverse.shape[0]):
        operator[i] = as_left(times(inverse[i], first[i, 0]))


def leaf_root_part_kernel(
    links,
    place,
    one,
    two,
    three,
    inverse,
    solved,
    mine,
    other,
    sep_own,
    part,
    root_sol,
    sep_rows,
    right,
):
    step = pl.program_id(0)
    count = root_sol.shape[0]

    @pl.when(step == 0)
    def _():
        is_first = place[1] == 0
        for r in range(count):
            root_sol[r, :, :128], root_sol[r, :, 128:] = halves(is_first, mine[r], other[r])
            right[r] = as_right(root_sol[r])
        sep_rows[0, :, :128], sep_rows[0, :, 128:] = halves(is_first, sep_own[...], other[count])

    batch = solved.shape[0]
    rests = []
    for i in range(batch):
        leaf = step * batch + i
        blocks = jnp.concatenate([one[i, 0], two[i, 0], three[i, 0]], axis=1)
        linked = jnp.concatenate([right[links[n, leaf] - 3] for n in (1, 2, 3)], axis=0)
        rests.append(solved[i] - left_times(as_left(blocks), linked))
    for i in range(batch):
        part[i] = times(inverse[i], rests[i])


def leaf_final_kernel(
    links,
    place,
    operator,
    part,
    own,
    other,
    far,
    far_other,
    near,
    near_other,
    out,
    seps,
    ready,
    sems,
):
    is_first = place[1] == 0
    last = other[other.shape[0] - 1]
    for t, (a, b) in enumerate(
        ((own[...], last), (near[...], near_other[...]), (far[...], far_other[...]))
    ):
        first, second = halves(is_first, a, b)
        seps[t, :, :128] = as_right(first)
        seps[t, :, 128:] = as_right(second)
    count = part.shape[0]
    copies = []
    for i in range(count):
        ready[i] = part[i] - left_times(operator[i], seps[links[0, i]])
        if i % 2 == 1:
            pair = pl.ds(i - 1, 2)
            copy = pltpu.make_async_copy(ready.at[pair], out.at[pair], sems.at[i // 2])
            copy.start()
            copies.append(copy)
    for copy in copies:
        copy.wait()


def whole(memory=VMEM):
    return pl.BlockSpec(memory_space=memory)


ANY = pl.BlockSpec(memory_space=pl.ANY)


def limit(megabytes):
    return pltpu.CompilerParams(vmem_limit_bytes=megabytes * 1024 * 1024)


def leafwise(batch, *tail):
    return pl.BlockSpec((batch,) + tail, lambda k: (k,) + (0,) * len(tail))


def link(batch, n, w):
    return pl.BlockSpec((batch, 1, w, w), lambda k: (k, n, 0, 0))


def kept(*shape):
    return pl.BlockSpec(shape, lambda k: (0,) * len(shape))


def per_device(
    leaf_rhs,
    leaf_lower_inverse,
    leaf_upper_inverse,
    leaf_lower,
    leaf_upper,
    leaf_rows,
    separator_right_sides,
    separator_lower_inverse,
    separator_upper_inverse,
    separator_lower_blocks,
    sep_upper,
    sep_rows,
    root_rhs,
    root_lower_inverse,
    root_upper_inverse,
    root_lower,
    root_upper,
):
    peers = lax.axis_size("grid")
    leaves, w, columns = leaf_rhs.shape
    roots = root_rhs.shape[0]
    half = columns // 2
    batch = leaves // 2
    position = lax.axis_index("grid") % 4
    core = lax.axis_index("layer")
    place = jnp.stack([position, core]).astype(jnp.int32)
    leaf_links = leaf_rows.T
    sep_links = sep_rows.reshape(-1)

    def shifted(x, by, to_other=0):
        pairs = [
            (2 * i + c, 2 * ((i + by) % peers) + (c ^ to_other))
            for i in range(peers)
            for c in range(2)
        ]
        return lax.ppermute(x, ("grid", "layer"), pairs)

    def crossed(x, bit):
        return lax.ppermute(x, "grid", [(i, i ^ bit) for i in range(peers)])

    def swapped(x):
        return lax.ppermute(x, "layer", [(0, 1), (1, 0)])

    shape = jax.ShapeDtypeStruct
    half_block = shape((w, half), F32)
    smem = whole(SMEM)

    leaf_solved, own, far, near = pl.pallas_call(
        forward_leaf_kernel,
        grid=(leaves // batch,),
        in_specs=[
            whole(SMEM),
            leafwise(batch, w, columns),
            leafwise(batch, w, w),
            link(batch, 0, w),
        ],
        out_specs=[leafwise(batch, w, columns)] + [kept(w, columns)] * 3,
        out_shape=[shape((leaves, w, columns), F32)] + [shape((w, columns), F32)] * 3,
        scratch_shapes=[VMEM((3, w, columns), F32)],
        compiler_params=limit(56),
        cost_estimate=cost(4),
        name="leaf_forward",
    )(leaf_links, leaf_rhs, leaf_lower_inverse, leaf_lower)

    far_sum = shifted(far, -(peers // 2))
    near_sum = shifted(near, -1)

    root_pending = pl.pallas_call(
        root_terms_kernel,
        grid=(leaves // batch,),
        in_specs=[
            whole(SMEM),
            link(batch, 1, w),
            link(batch, 2, w),
            link(batch, 3, w),
            leafwise(batch, w, columns),
        ],
        out_specs=kept(roots, w, columns),
        out_shape=shape((roots, w, columns), F32),
        compiler_params=limit(16),
        cost_estimate=cost(3),
        name="root_terms",
    )(leaf_links, leaf_lower, leaf_lower, leaf_lower, leaf_solved)

    sep_forward = pl.pallas_call(
        separator_operator_kernel,
        in_specs=[whole()] * 2 + [ANY],
        out_specs=whole(),
        out_shape=shape((6 * w, 2 * w), BF16),
        compiler_params=limit(16),
        cost_estimate=cost(0.5),
        name="separator_operator",
    )(separator_lower_inverse, separator_lower_blocks, leaf_solved)

    sep_right, mine, theirs = pl.pallas_call(
        separator_kernel,
        in_specs=[whole(SMEM), whole(SMEM)] + [whole()] * 6,
        out_specs=[whole()] * 3,
        out_shape=[
            shape((2 * w, columns), BF16),
            shape((roots, w, half), F32),
            shape((roots, w, half), F32),
        ],
        scratch_shapes=[VMEM((roots, w, columns), F32)],
        compiler_params=limit(16),
        cost_estimate=cost(2),
        name="separator_forward",
    )(
        sep_links,
        place,
        separator_right_sides,
        sep_forward,
        own,
        far_sum,
        near_sum,
        root_pending,
    )

    other = swapped(theirs)
    sep_mine, sep_pack = pl.pallas_call(
        separator_part_kernel,
        in_specs=[smem] * 2 + [whole()] * 4,
        out_specs=[whole()] * 2,
        out_shape=[half_block, shape((roots + 1, w, half), F32)],
        compiler_params=limit(16),
        cost_estimate=cost(0.7),
        name="separator_part",
    )(
        sep_links,
        place,
        separator_lower_inverse,
        separator_upper_inverse,
        sep_upper,
        sep_right,
    )
    other_pack = swapped(sep_pack)
    sep_backward = pl.pallas_call(
        separator_factors_kernel,
        in_specs=[whole()] * 2,
        out_specs=whole(),
        out_shape=shape((2, 2 * w, 2 * roots * w), BF16),
        compiler_params=limit(16),
        cost_estimate=cost(0.2),
        name="separator_factors",
    )(sep_pack, other_pack)
    pieces = [mine[j] + other[j] for j in range(4)]
    forward, backward = pl.pallas_call(
        root_sweeps_kernel,
        in_specs=[whole()] * 4 + [ANY],
        out_specs=[whole()] * 2,
        out_shape=[shape((roots * w, roots * w), F32)] * 2,
        compiler_params=limit(16),
        cost_estimate=cost(2.3),
        name="root_sweeps",
    )(root_lower_inverse, root_upper_inverse, root_lower, root_upper, pieces[1])
    arrived = [crossed(pieces[j], j) for j in (3, 2, 1)]
    arrived, forward, backward = lax.optimization_barrier((arrived, forward, backward))
    total = pieces[0] + arrived[0] + arrived[1] + arrived[2]

    root_operator = pl.pallas_call(
        root_operator_kernel,
        in_specs=[whole()] * 2 + [ANY],
        out_specs=whole(),
        out_shape=shape((2 * roots * w, 2 * roots * w), BF16),
        compiler_params=limit(16),
        cost_estimate=cost(1),
        name="root_operator",
    )(forward, backward, total)

    bit = 4
    while bit < peers:
        arrived = crossed(total, bit)
        if bit == 4:
            arrived, root_operator = lax.optimization_barrier((arrived, root_operator))
        total = total + arrived
        bit *= 2
    others = [crossed(total, j) for j in (3, 2, 1)]

    solution_half, sep_own, sep_other = pl.pallas_call(
        root_kernel,
        in_specs=[smem] + [whole()] * 9,
        out_specs=[whole()] * 3,
        out_shape=[shape((roots + 1, w, half), F32)] + [half_block] * 2,
        scratch_shapes=[VMEM((2 * roots * w, half), BF16)] * 2,
        compiler_params=limit(16),
        cost_estimate=cost(2),
        name="root_solve",
    )(
        place,
        root_rhs,
        root_operator,
        *others,
        total,
        sep_backward,
        sep_mine,
        other_pack,
    )

    far_rows = shifted(sep_own, peers // 2)
    far_other_rows = shifted(sep_other, peers // 2, 1)
    near_rows = shifted(sep_own, 1)
    near_other_rows = shifted(sep_other, 1, 1)
    other_half = swapped(solution_half)

    leaf_operator = pl.pallas_call(
        leaf_operator_kernel,
        grid=(leaves // batch,),
        in_specs=[leafwise(batch, w, w), link(batch, 0, w), ANY],
        out_specs=leafwise(batch, 2 * w, 2 * w),
        out_shape=shape((leaves, 2 * w, 2 * w), BF16),
        compiler_params=limit(16),
        cost_estimate=cost(1),
        name="leaf_operators",
    )(leaf_upper_inverse, leaf_upper, sep_own)

    leaf_part, root_sol, separator_solution_rows = pl.pallas_call(
        leaf_root_part_kernel,
        grid=(leaves // batch,),
        in_specs=[
            smem,
            smem,
            link(batch, 1, w),
            link(batch, 2, w),
            link(batch, 3, w),
            leafwise(batch, w, w),
            leafwise(batch, w, columns),
            kept(roots + 1, w, half),
            kept(roots + 1, w, half),
            kept(w, half),
        ],
        out_specs=[
            leafwise(batch, w, columns),
            kept(roots, w, columns),
            kept(1, w, columns),
        ],
        out_shape=[
            shape((leaves, w, columns), F32),
            shape((roots, w, columns), F32),
            shape((1, w, columns), F32),
        ],
        scratch_shapes=[VMEM((roots, 2 * w, columns), BF16)],
        compiler_params=limit(16),
        cost_estimate=cost(3),
        name="leaf_root_part",
    )(
        leaf_links,
        place,
        leaf_upper,
        leaf_upper,
        leaf_upper,
        leaf_upper_inverse,
        leaf_solved,
        solution_half,
        other_half,
        sep_own,
    )

    leaf_sol = pl.pallas_call(
        leaf_final_kernel,
        in_specs=[smem] * 2 + [whole()] * 8,
        out_specs=ANY,
        out_shape=shape((leaves, w, columns), F32),
        scratch_shapes=[
            VMEM((3, 2 * w, columns), BF16),
            VMEM((leaves, w, columns), F32),
            pltpu.SemaphoreType.DMA((leaves // 2,)),
        ],
        compiler_params=limit(16),
        cost_estimate=cost(2),
        name="leaf_backward",
    )(
        leaf_links,
        place,
        leaf_operator,
        leaf_part,
        sep_own,
        other_half,
        far_rows,
        far_other_rows,
        near_rows,
        near_other_rows,
    )
    return (leaf_sol, separator_solution_rows, root_sol)


def solution(mesh):
    by_device = P(("groups", "grid", "layer"))
    by_group = P("groups")
    return jax.shard_map(
        per_device,
        mesh=mesh,
        in_specs=(by_device,) * 12 + (by_group,) * 5,
        out_specs=(by_device, by_device, by_group),
        check_vma=False,
    )
```

```python
import functools

import jax
import jax.numpy as jnp
from jax import lax
from jax.experimental import pallas as pl
from jax.experimental.pallas import tpu as pltpu
from jax.sharding import PartitionSpec as P

VMEM = pltpu.VMEM
SMEM = pltpu.SMEM
F32 = jnp.float32
BF16 = jnp.bfloat16


def parts_of(x):
    high = x.astype(BF16)
    low = (x - high.astype(F32)).astype(BF16)
    return high, low


def as_left(x):
    high, low = parts_of(x)
    count = x.shape[1] // 128
    pieces = [slice(j * 128, j * 128 + 128) for j in range(count)]
    top = jnp.concatenate([high[:, s] for s in pieces for _ in range(2)], axis=1)
    bottom = jnp.concatenate([low[:, s] for s in pieces for _ in range(2)], axis=1)
    return jnp.concatenate([top, bottom], axis=0)


def as_right(x):
    high, low = parts_of(x)
    count = x.shape[0] // 128
    pieces = [slice(j * 128, j * 128 + 128) for j in range(count)]
    return jnp.concatenate([y[s] for s in pieces for y in (high, low)], axis=0)


def left_times(left, right):
    both = jnp.dot(left, right, preferred_element_type=F32)
    rows = left.shape[0] // 2
    return both[:rows] + both[rows:]


def times(a, b):
    return left_times(as_left(a), as_right(b))


def halves(is_first, mine, other):
    return jnp.where(is_first, mine, other), jnp.where(is_first, other, mine)


def cost(microseconds):
    return pl.CostEstimate(
        flops=int(microseconds * 1e9),
        bytes_accessed=int(microseconds * 3e6),
        transcendentals=0,
    )


def forward_leaf_kernel(links, rhs, inverse, first, solved, own, far, near, pending):
    step = pl.program_id(0)

    @pl.when(step == 0)
    def _():
        pending[...] = jnp.zeros_like(pending)

    batch = rhs.shape[0]
    values = []
    for i in range(batch):
        value = times(inverse[i], rhs[i])
        solved[i] = value
        values.append(value)
    for i in range(batch):
        pending[links[0, step * batch + i]] += times(first[i, 0], values[i])

    @pl.when(step == pl.num_programs(0) - 1)
    def _():
        own[...] = pending[0]
        near[...] = pending[1]
        far[...] = pending[2]


def root_terms_kernel(links, one, two, three, solved, pending):
    step = pl.program_id(0)

    @pl.when(step == 0)
    def _():
        pending[...] = jnp.zeros_like(pending)

    batch = solved.shape[0]
    for i in range(batch):
        blocks = jnp.concatenate([one[i, 0], two[i, 0], three[i, 0]], axis=0)
        terms = times(blocks, solved[i])
        for n in range(3):
            slot = links[n + 1, step * batch + i] - 3
            pending[slot] += terms[n * 128 : n * 128 + 128]


def root_sweeps_kernel(lower_inverse, upper_inverse, lower, upper, after, forward, backward):
    count = lower_inverse.shape[0]
    w = lower_inverse.shape[1]
    forward[...] = jnp.zeros_like(forward)
    backward[...] = jnp.zeros_like(backward)
    for step in range(count):
        r = step
        here = slice(r * w, r * w + w)
        forward[here, here] = lower_inverse[r]
        if step > 0:
            done = slice(0, r * w)
            inner = times(lower[here, done], forward[done, done])
            forward[here, done] = -times(lower_inverse[r], inner)
        r = count - 1 - step
        here = slice(r * w, r * w + w)
        backward[here, here] = upper_inverse[r]
        if step > 0:
            done = slice((r + 1) * w, count * w)
            inner = times(upper[here, done], backward[done, done])
            backward[here, done] = -times(upper_inverse[r], inner)


def root_operator_kernel(forward, backward, after, root_operator, root_right):
    w = 128
    size = forward.shape[0]
    for r in range(0, size, w):
        block = times(backward[r : r + w, r:], forward[r:, :])
        root_right[2 * r : 2 * r + 2 * w, :] = as_right(block)
        left = as_left(block)
        root_operator[r : r + w, :] = left[:w]
        root_operator[size + r : size + r + w, :] = left[w:]


def separator_operator_kernel(lower_inverse, lower, after, forward):
    blocks = jnp.concatenate([lower[0, n] for n in range(3)], axis=0)
    forward[...] = as_left(times(blocks, lower_inverse[0]))


def separator_kernel(
    links, place, rhs, operator, own, far, near, root_pending, right, mine, theirs, sums
):
    right[...] = as_right(rhs[0] - own[...] - near[...] - far[...])
    terms = left_times(operator[...], right[...])
    sums[...] = root_pending[...]
    for n in range(3):
        sums[links[n]] += terms[n * 128 : n * 128 + 128]
    position = place[0]
    is_first = place[1] == 0
    for j in range(4):
        block = sums[position ^ j]
        first, second = block[:, :128], block[:, 128:]
        mine[j] = jnp.where(is_first, first, second)
        theirs[j] = jnp.where(is_first, second, first)


def separator_part_kernel(
    links, place, lower_inverse, upper_inverse, upper, right, mine, pack
):
    blocks = jnp.concatenate([upper[0, n] for n in range(3)], axis=1)
    back = times(upper_inverse[0], blocks)
    last = pack.shape[0] - 1
    pack[...] = jnp.zeros_like(pack)
    for n in range(3):
        pack[links[n]] = back[:, n * 128 : n * 128 + 128]
    operator = as_left(times(upper_inverse[0], lower_inverse[0]))
    part = left_times(operator, right[...])
    mine[...], pack[last] = halves(place[1] == 0, part[:, :128], part[:, 128:])


def separator_factors_kernel(pack, other, root_right, backward):
    for i, blocks in enumerate((pack, other)):
        row = jnp.concatenate([blocks[r] for r in range(blocks.shape[0] - 1)], axis=1)
        backward[i] = as_left(left_times(as_left(row), root_right[...]))


def root_kernel(
    place,
    rhs,
    operator,
    three,
    two,
    one,
    own,
    backward,
    part,
    other_pack,
    out,
    sep_own,
    sep_other,
    pending,
):
    count, w = rhs.shape[0], rhs.shape[1]
    position = place[0]
    is_first = place[1] == 0
    for j, piece in enumerate((own, one, two, three)):
        root = position ^ j
        side = rhs[root]
        side = jnp.where(is_first, side[:, :128], side[:, 128:])
        pending[pl.ds(pl.multiple_of(root * 2 * w, 2 * w), 2 * w), :] = as_right(
            side - piece[...]
        )
    solution = left_times(operator[...], pending[...])
    for r in range(count):
        out[r] = solution[r * w : r * w + w]
    sep_own[...] = part[...] - left_times(backward[0], pending[...])
    sep_other[...] = other_pack[count] - left_times(backward[1], pending[...])
    out[count] = sep_other[...]


def leaf_operator_kernel(inverse, first, after, operator):
    for i in range(inverse.shape[0]):
        operator[i] = as_left(times(inverse[i], first[i, 0]))


def leaf_root_part_kernel(
    links,
    place,
    one,
    two,
    three,
    inverse,
    solved,
    mine,
    other,
    sep_own,
    part,
    root_sol,
    sep_rows,
    right,
):
    step = pl.program_id(0)
    count = root_sol.shape[0]

    @pl.when(step == 0)
    def _():
        is_first = place[1] == 0
        for r in range(count):
            root_sol[r, :, :128], root_sol[r, :, 128:] = halves(is_first, mine[r], other[r])
            right[r] = as_right(root_sol[r])
        sep_rows[0, :, :128], sep_rows[0, :, 128:] = halves(is_first, sep_own[...], other[count])

    batch = solved.shape[0]
    rests = []
    for i in range(batch):
        leaf = step * batch + i
        blocks = jnp.concatenate([one[i, 0], two[i, 0], three[i, 0]], axis=1)
        linked = jnp.concatenate([right[links[n, leaf] - 3] for n in (1, 2, 3)], axis=0)
        rests.append(solved[i] - left_times(as_left(blocks), linked))
    for i in range(batch):
        part[i] = times(inverse[i], rests[i])


def leaf_final_kernel(
    links,
    place,
    operator,
    part,
    own,
    other,
    far,
    far_other,
    near,
    near_other,
    out,
    seps,
    ready,
    sems,
):
    is_first = place[1] == 0
    last = other[other.shape[0] - 1]
    for t, (a, b) in enumerate(
        ((own[...], last), (near[...], near_other[...]), (far[...], far_other[...]))
    ):
        first, second = halves(is_first, a, b)
        seps[t, :, :128] = as_right(first)
        seps[t, :, 128:] = as_right(second)
    count = part.shape[0]
    copies = []
    for i in range(count):
        ready[i] = part[i] - left_times(operator[i], seps[links[0, i]])
        if i % 2 == 1:
            pair = pl.ds(i - 1, 2)
            copy = pltpu.make_async_copy(ready.at[pair], out.at[pair], sems.at[i // 2])
            copy.start()
            copies.append(copy)
    for copy in copies:
        copy.wait()


def whole(memory=VMEM):
    return pl.BlockSpec(memory_space=memory)


ANY = pl.BlockSpec(memory_space=pl.ANY)


def limit(megabytes):
    return pltpu.CompilerParams(vmem_limit_bytes=megabytes * 1024 * 1024)


def leafwise(batch, *tail):
    return pl.BlockSpec((batch,) + tail, lambda k: (k,) + (0,) * len(tail))


def link(batch, n, w):
    return pl.BlockSpec((batch, 1, w, w), lambda k: (k, n, 0, 0))


def kept(*shape):
    return pl.BlockSpec(shape, lambda k: (0,) * len(shape))


def per_device(
    leaf_rhs,
    leaf_lower_inverse,
    leaf_upper_inverse,
    leaf_lower,
    leaf_upper,
    leaf_rows,
    separator_right_sides,
    separator_lower_inverse,
    separator_upper_inverse,
    separator_lower_blocks,
    sep_upper,
    sep_rows,
    root_rhs,
    root_lower_inverse,
    root_upper_inverse,
    root_lower,
    root_upper,
):
    peers = lax.axis_size("grid")
    leaves, w, columns = leaf_rhs.shape
    roots = root_rhs.shape[0]
    half = columns // 2
    batch = leaves // 2
    position = lax.axis_index("grid") % 4
    core = lax.axis_index("layer")
    place = jnp.stack([position, core]).astype(jnp.int32)
    leaf_links = leaf_rows.T
    sep_links = sep_rows.reshape(-1)

    def shifted(x, by, to_other=0):
        pairs = [
            (2 * i + c, 2 * ((i + by) % peers) + (c ^ to_other))
            for i in range(peers)
            for c in range(2)
        ]
        return lax.ppermute(x, ("grid", "layer"), pairs)

    def crossed(x, bit):
        return lax.ppermute(x, "grid", [(i, i ^ bit) for i in range(peers)])

    def swapped(x):
        return lax.ppermute(x, "layer", [(0, 1), (1, 0)])

    shape = jax.ShapeDtypeStruct
    half_block = shape((w, half), F32)
    smem = whole(SMEM)

    leaf_solved, own, far, near = pl.pallas_call(
        forward_leaf_kernel,
        grid=(leaves // batch,),
        in_specs=[
            whole(SMEM),
            leafwise(batch, w, columns),
            leafwise(batch, w, w),
            link(batch, 0, w),
        ],
        out_specs=[leafwise(batch, w, columns)] + [kept(w, columns)] * 3,
        out_shape=[shape((leaves, w, columns), F32)] + [shape((w, columns), F32)] * 3,
        scratch_shapes=[VMEM((3, w, columns), F32)],
        compiler_params=limit(56),
        cost_estimate=cost(4),
        name="leaf_forward",
    )(leaf_links, leaf_rhs, leaf_lower_inverse, leaf_lower)

    far_sum = shifted(far, -(peers // 2))
    near_sum = shifted(near, -1)

    root_pending = pl.pallas_call(
        root_terms_kernel,
        grid=(leaves // batch,),
        in_specs=[
            whole(SMEM),
            link(batch, 1, w),
            link(batch, 2, w),
            link(batch, 3, w),
            leafwise(batch, w, columns),
        ],
        out_specs=kept(roots, w, columns),
        out_shape=shape((roots, w, columns), F32),
        compiler_params=limit(16),
        cost_estimate=cost(3),
        name="root_terms",
    )(leaf_links, leaf_lower, leaf_lower, leaf_lower, leaf_solved)

    sep_forward = pl.pallas_call(
        separator_operator_kernel,
        in_specs=[whole()] * 2 + [ANY],
        out_specs=whole(),
        out_shape=shape((6 * w, 2 * w), BF16),
        compiler_params=limit(16),
        cost_estimate=cost(0.5),
        name="separator_operator",
    )(separator_lower_inverse, separator_lower_blocks, leaf_solved)

    sep_right, mine, theirs = pl.pallas_call(
        separator_kernel,
        in_specs=[whole(SMEM), whole(SMEM)] + [whole()] * 6,
        out_specs=[whole()] * 3,
        out_shape=[
            shape((2 * w, columns), BF16),
            shape((roots, w, half), F32),
            shape((roots, w, half), F32),
        ],
        scratch_shapes=[VMEM((roots, w, columns), F32)],
        compiler_params=limit(16),
        cost_estimate=cost(2),
        name="separator_forward",
    )(
        sep_links,
        place,
        separator_right_sides,
        sep_forward,
        own,
        far_sum,
        near_sum,
        root_pending,
    )

    other = swapped(theirs)
    sep_mine, sep_pack = pl.pallas_call(
        separator_part_kernel,
        in_specs=[smem] * 2 + [whole()] * 4,
        out_specs=[whole()] * 2,
        out_shape=[half_block, shape((roots + 1, w, half), F32)],
        compiler_params=limit(16),
        cost_estimate=cost(0.7),
        name="separator_part",
    )(
        sep_links,
        place,
        separator_lower_inverse,
        separator_upper_inverse,
        sep_upper,
        sep_right,
    )
    other_pack = swapped(sep_pack)
    pieces = [mine[j] + other[j] for j in range(4)]
    forward, backward = pl.pallas_call(
        root_sweeps_kernel,
        in_specs=[whole()] * 4 + [ANY],
        out_specs=[whole()] * 2,
        out_shape=[shape((roots * w, roots * w), F32)] * 2,
        compiler_params=limit(16),
        cost_estimate=cost(2.3),
        name="root_sweeps",
    )(root_lower_inverse, root_upper_inverse, root_lower, root_upper, pieces[1])
    arrived = [crossed(pieces[j], j) for j in (3, 2, 1)]
    arrived, forward, backward = lax.optimization_barrier((arrived, forward, backward))
    total = pieces[0] + arrived[0] + arrived[1] + arrived[2]

    root_operator, root_right = pl.pallas_call(
        root_operator_kernel,
        in_specs=[whole()] * 2 + [ANY],
        out_specs=[whole()] * 2,
        out_shape=[
            shape((2 * roots * w, 2 * roots * w), BF16),
            shape((2 * roots * w, roots * w), BF16),
        ],
        compiler_params=limit(16),
        cost_estimate=cost(1),
        name="root_operator",
    )(forward, backward, total)

    bit = 4
    while bit < peers:
        arrived = crossed(total, bit)
        if bit == 4:
            arrived, root_operator = lax.optimization_barrier((arrived, root_operator))
        total = total + arrived
        bit *= 2
    sep_backward = pl.pallas_call(
        separator_factors_kernel,
        in_specs=[whole()] * 3,
        out_specs=whole(),
        out_shape=shape((2, 2 * w, 2 * roots * w), BF16),
        compiler_params=limit(16),
        cost_estimate=cost(0.5),
        name="separator_factors",
    )(sep_pack, other_pack, root_right)
    others = [crossed(total, j) for j in (3, 2, 1)]

    solution_half, sep_own, sep_other = pl.pallas_call(
        root_kernel,
        in_specs=[smem] + [whole()] * 9,
        out_specs=[whole()] * 3,
        out_shape=[shape((roots + 1, w, half), F32)] + [half_block] * 2,
        scratch_shapes=[VMEM((2 * roots * w, half), BF16)],
        compiler_params=limit(16),
        cost_estimate=cost(2),
        name="root_solve",
    )(
        place,
        root_rhs,
        root_operator,
        *others,
        total,
        sep_backward,
        sep_mine,
        other_pack,
    )

    far_rows = shifted(sep_own, peers // 2)
    far_other_rows = shifted(sep_other, peers // 2, 1)
    near_rows = shifted(sep_own, 1)
    near_other_rows = shifted(sep_other, 1, 1)
    other_half = swapped(solution_half)

    leaf_operator = pl.pallas_call(
        leaf_operator_kernel,
        grid=(leaves // batch,),
        in_specs=[leafwise(batch, w, w), link(batch, 0, w), ANY],
        out_specs=leafwise(batch, 2 * w, 2 * w),
        out_shape=shape((leaves, 2 * w, 2 * w), BF16),
        compiler_params=limit(16),
        cost_estimate=cost(1),
        name="leaf_operators",
    )(leaf_upper_inverse, leaf_upper, sep_own)

    leaf_part, root_sol, separator_solution_rows = pl.pallas_call(
        leaf_root_part_kernel,
        grid=(leaves // batch,),
        in_specs=[
            smem,
            smem,
            link(batch, 1, w),
            link(batch, 2, w),
            link(batch, 3, w),
            leafwise(batch, w, w),
            leafwise(batch, w, columns),
            kept(roots + 1, w, half),
            kept(roots + 1, w, half),
            kept(w, half),
        ],
        out_specs=[
            leafwise(batch, w, columns),
            kept(roots, w, columns),
            kept(1, w, columns),
        ],
        out_shape=[
            shape((leaves, w, columns), F32),
            shape((roots, w, columns), F32),
            shape((1, w, columns), F32),
        ],
        scratch_shapes=[VMEM((roots, 2 * w, columns), BF16)],
        compiler_params=limit(16),
        cost_estimate=cost(3),
        name="leaf_root_part",
    )(
        leaf_links,
        place,
        leaf_upper,
        leaf_upper,
        leaf_upper,
        leaf_upper_inverse,
        leaf_solved,
        solution_half,
        other_half,
        sep_own,
    )

    leaf_sol = pl.pallas_call(
        leaf_final_kernel,
        in_specs=[smem] * 2 + [whole()] * 8,
        out_specs=ANY,
        out_shape=shape((leaves, w, columns), F32),
        scratch_shapes=[
            VMEM((3, 2 * w, columns), BF16),
            VMEM((leaves, w, columns), F32),
            pltpu.SemaphoreType.DMA((leaves // 2,)),
        ],
        compiler_params=limit(16),
        cost_estimate=cost(2),
        name="leaf_backward",
    )(
        leaf_links,
        place,
        leaf_operator,
        leaf_part,
        sep_own,
        other_half,
        far_rows,
        far_other_rows,
        near_rows,
        near_other_rows,
    )
    return (leaf_sol, separator_solution_rows, root_sol)


def solution(mesh):
    by_device = P(("groups", "grid", "layer"))
    by_group = P("groups")
    return jax.shard_map(
        per_device,
        mesh=mesh,
        in_specs=(by_device,) * 12 + (by_group,) * 5,
        out_specs=(by_device, by_device, by_group),
        check_vma=False,
    )
```

```python
import functools

import jax
import jax.numpy as jnp
from jax import lax
from jax.experimental import pallas as pl
from jax.experimental.pallas import tpu as pltpu
from jax.sharding import PartitionSpec as P

VMEM = pltpu.VMEM
SMEM = pltpu.SMEM
F32 = jnp.float32
BF16 = jnp.bfloat16


def parts_of(x):
    high = x.astype(BF16)
    low = (x - high.astype(F32)).astype(BF16)
    return high, low


def as_left(x):
    high, low = parts_of(x)
    count = x.shape[1] // 128
    pieces = [slice(j * 128, j * 128 + 128) for j in range(count)]
    top = jnp.concatenate([high[:, s] for s in pieces for _ in range(2)], axis=1)
    bottom = jnp.concatenate([low[:, s] for s in pieces for _ in range(2)], axis=1)
    return jnp.concatenate([top, bottom], axis=0)


def as_right(x):
    high, low = parts_of(x)
    count = x.shape[0] // 128
    pieces = [slice(j * 128, j * 128 + 128) for j in range(count)]
    return jnp.concatenate([y[s] for s in pieces for y in (high, low)], axis=0)


def left_times(left, right):
    both = jnp.dot(left, right, preferred_element_type=F32)
    rows = left.shape[0] // 2
    return both[:rows] + both[rows:]


def times(a, b):
    return left_times(as_left(a), as_right(b))


def halves(is_first, mine, other):
    return jnp.where(is_first, mine, other), jnp.where(is_first, other, mine)


def cost(microseconds):
    return pl.CostEstimate(
        flops=int(microseconds * 1e9),
        bytes_accessed=int(microseconds * 3e6),
        transcendentals=0,
    )


def forward_leaf_kernel(links, rhs, inverse, first, solved, own, far, near, pending):
    step = pl.program_id(0)

    @pl.when(step == 0)
    def _():
        pending[...] = jnp.zeros_like(pending)

    batch = rhs.shape[0]
    values = []
    for i in range(batch):
        value = times(inverse[i], rhs[i])
        solved[i] = value
        values.append(value)
    for i in range(batch):
        pending[links[0, step * batch + i]] += times(first[i, 0], values[i])

    @pl.when(step == pl.num_programs(0) - 1)
    def _():
        own[...] = pending[0]
        near[...] = pending[1]
        far[...] = pending[2]


def root_terms_kernel(links, one, two, three, solved, pending):
    step = pl.program_id(0)

    @pl.when(step == 0)
    def _():
        pending[...] = jnp.zeros_like(pending)

    batch = solved.shape[0]
    for i in range(batch):
        blocks = jnp.concatenate([one[i, 0], two[i, 0], three[i, 0]], axis=0)
        terms = times(blocks, solved[i])
        for n in range(3):
            slot = links[n + 1, step * batch + i] - 3
            pending[slot] += terms[n * 128 : n * 128 + 128]


def root_sweeps_kernel(lower_inverse, upper_inverse, lower, upper, after, forward, backward):
    count = lower_inverse.shape[0]
    w = lower_inverse.shape[1]
    forward[...] = jnp.zeros_like(forward)
    backward[...] = jnp.zeros_like(backward)
    for step in range(count):
        r = step
        here = slice(r * w, r * w + w)
        forward[here, here] = lower_inverse[r]
        if step > 0:
            done = slice(0, r * w)
            inner = times(lower[here, done], forward[done, done])
            forward[here, done] = -times(lower_inverse[r], inner)
        r = count - 1 - step
        here = slice(r * w, r * w + w)
        backward[here, here] = upper_inverse[r]
        if step > 0:
            done = slice((r + 1) * w, count * w)
            inner = times(upper[here, done], backward[done, done])
            backward[here, done] = -times(upper_inverse[r], inner)


def root_operator_kernel(forward, backward, after, root_operator, root_right):
    w = 128
    size = forward.shape[0]
    for r in range(0, size, w):
        block = times(backward[r : r + w, r:], forward[r:, :])
        root_right[2 * r : 2 * r + 2 * w, :] = as_right(block)
        left = as_left(block)
        root_operator[r : r + w, :] = left[:w]
        root_operator[size + r : size + r + w, :] = left[w:]


def separator_operator_kernel(lower_inverse, lower, after, forward):
    blocks = jnp.concatenate([lower[0, n] for n in range(3)], axis=0)
    forward[...] = as_left(times(blocks, lower_inverse[0]))


def separator_kernel(
    links, place, rhs, operator, own, far, near, root_pending, right, mine, theirs, sums
):
    right[...] = as_right(rhs[0] - own[...] - near[...] - far[...])
    terms = left_times(operator[...], right[...])
    sums[...] = root_pending[...]
    for n in range(3):
        sums[links[n]] += terms[n * 128 : n * 128 + 128]
    position = place[0]
    is_first = place[1] == 0
    for j in range(4):
        block = sums[position ^ j]
        first, second = block[:, :128], block[:, 128:]
        mine[j] = jnp.where(is_first, first, second)
        theirs[j] = jnp.where(is_first, second, first)


def separator_part_kernel(
    links, place, lower_inverse, upper_inverse, upper, right, mine, pack
):
    blocks = jnp.concatenate([upper[0, n] for n in range(3)], axis=1)
    back = times(upper_inverse[0], blocks)
    last = pack.shape[0] - 1
    pack[...] = jnp.zeros_like(pack)
    for n in range(3):
        pack[links[n]] = back[:, n * 128 : n * 128 + 128]
    operator = as_left(times(upper_inverse[0], lower_inverse[0]))
    part = left_times(operator, right[...])
    mine[...], pack[last] = halves(place[1] == 0, part[:, :128], part[:, 128:])


def separator_factors_kernel(pack, other, root_right, backward):
    for i, blocks in enumerate((pack, other)):
        row = jnp.concatenate([blocks[r] for r in range(blocks.shape[0] - 1)], axis=1)
        backward[i] = as_left(left_times(as_left(row), root_right[...]))


def root_kernel(
    place,
    rhs,
    operator,
    three,
    two,
    one,
    own,
    backward,
    part,
    other_pack,
    out,
    sep_own,
    sep_other,
    own_again,
    other_again,
    pending,
):
    count, w = rhs.shape[0], rhs.shape[1]
    position = place[0]
    is_first = place[1] == 0
    for j, piece in enumerate((own, one, two, three)):
        root = position ^ j
        side = rhs[root]
        side = jnp.where(is_first, side[:, :128], side[:, 128:])
        pending[pl.ds(pl.multiple_of(root * 2 * w, 2 * w), 2 * w), :] = as_right(
            side - piece[...]
        )
    solution = left_times(operator[...], pending[...])
    for r in range(count):
        out[r] = solution[r * w : r * w + w]
    sep_own[...] = part[...] - left_times(backward[0], pending[...])
    sep_other[...] = other_pack[count] - left_times(backward[1], pending[...])
    out[count] = sep_other[...]
    own_again[...] = sep_own[...]
    other_again[...] = sep_other[...]


def leaf_operator_kernel(inverse, first, after, operator):
    for i in range(inverse.shape[0]):
        operator[i] = as_left(times(inverse[i], first[i, 0]))


def leaf_root_part_kernel(
    links,
    place,
    one,
    two,
    three,
    inverse,
    solved,
    mine,
    other,
    sep_own,
    part,
    root_sol,
    sep_rows,
    right,
):
    step = pl.program_id(0)
    count = root_sol.shape[0]

    @pl.when(step == 0)
    def _():
        is_first = place[1] == 0
        for r in range(count):
            root_sol[r, :, :128], root_sol[r, :, 128:] = halves(is_first, mine[r], other[r])
            right[r] = as_right(root_sol[r])
        sep_rows[0, :, :128], sep_rows[0, :, 128:] = halves(is_first, sep_own[...], other[count])

    batch = solved.shape[0]
    rests = []
    for i in range(batch):
        leaf = step * batch + i
        blocks = jnp.concatenate([one[i, 0], two[i, 0], three[i, 0]], axis=1)
        linked = jnp.concatenate([right[links[n, leaf] - 3] for n in (1, 2, 3)], axis=0)
        rests.append(solved[i] - left_times(as_left(blocks), linked))
    for i in range(batch):
        part[i] = times(inverse[i], rests[i])


def leaf_final_kernel(
    links,
    place,
    operator,
    part,
    own,
    other,
    near,
    far,
    near_other,
    far_other,
    out,
    seps,
    ready,
    sems,
):
    is_first = place[1] == 0
    last = other[other.shape[0] - 1]
    for t, (a, b) in enumerate(
        ((own[...], last), (near[...], near_other[...]), (far[...], far_other[...]))
    ):
        first, second = halves(is_first, a, b)
        seps[t, :, :128] = as_right(first)
        seps[t, :, 128:] = as_right(second)
    count = part.shape[0]
    copies = []
    for i in range(count):
        ready[i] = part[i] - left_times(operator[i], seps[links[0, i]])
        if i % 2 == 1:
            pair = pl.ds(i - 1, 2)
            copy = pltpu.make_async_copy(ready.at[pair], out.at[pair], sems.at[i // 2])
            copy.start()
            copies.append(copy)
    for copy in copies:
        copy.wait()


def whole(memory=VMEM):
    return pl.BlockSpec(memory_space=memory)


ANY = pl.BlockSpec(memory_space=pl.ANY)


def limit(megabytes):
    return pltpu.CompilerParams(vmem_limit_bytes=megabytes * 1024 * 1024)


def leafwise(batch, *tail):
    return pl.BlockSpec((batch,) + tail, lambda k: (k,) + (0,) * len(tail))


def link(batch, n, w):
    return pl.BlockSpec((batch, 1, w, w), lambda k: (k, n, 0, 0))


def kept(*shape):
    return pl.BlockSpec(shape, lambda k: (0,) * len(shape))


def per_device(
    leaf_rhs,
    leaf_lower_inverse,
    leaf_upper_inverse,
    leaf_lower,
    leaf_upper,
    leaf_rows,
    separator_right_sides,
    separator_lower_inverse,
    separator_upper_inverse,
    separator_lower_blocks,
    sep_upper,
    sep_rows,
    root_rhs,
    root_lower_inverse,
    root_upper_inverse,
    root_lower,
    root_upper,
):
    peers = lax.axis_size("grid")
    leaves, w, columns = leaf_rhs.shape
    roots = root_rhs.shape[0]
    half = columns // 2
    batch = leaves // 2
    position = lax.axis_index("grid") % 4
    core = lax.axis_index("layer")
    place = jnp.stack([position, core]).astype(jnp.int32)
    leaf_links = leaf_rows.T
    sep_links = sep_rows.reshape(-1)

    def shifted(x, by, to_other=0):
        pairs = [
            (2 * i + c, 2 * ((i + by) % peers) + (c ^ to_other))
            for i in range(peers)
            for c in range(2)
        ]
        return lax.ppermute(x, ("grid", "layer"), pairs)

    def crossed(x, bit):
        return lax.ppermute(x, "grid", [(i, i ^ bit) for i in range(peers)])

    def swapped(x):
        return lax.ppermute(x, "layer", [(0, 1), (1, 0)])

    shape = jax.ShapeDtypeStruct
    half_block = shape((w, half), F32)
    smem = whole(SMEM)

    leaf_solved, own, far, near = pl.pallas_call(
        forward_leaf_kernel,
        grid=(leaves // batch,),
        in_specs=[
            whole(SMEM),
            leafwise(batch, w, columns),
            leafwise(batch, w, w),
            link(batch, 0, w),
        ],
        out_specs=[leafwise(batch, w, columns)] + [kept(w, columns)] * 3,
        out_shape=[shape((leaves, w, columns), F32)] + [shape((w, columns), F32)] * 3,
        scratch_shapes=[VMEM((3, w, columns), F32)],
        compiler_params=limit(56),
        cost_estimate=cost(4),
        name="leaf_forward",
    )(leaf_links, leaf_rhs, leaf_lower_inverse, leaf_lower)

    far_sum = shifted(far, -(peers // 2))
    near_sum = shifted(near, -1)

    root_pending = pl.pallas_call(
        root_terms_kernel,
        grid=(leaves // batch,),
        in_specs=[
            whole(SMEM),
            link(batch, 1, w),
            link(batch, 2, w),
            link(batch, 3, w),
            leafwise(batch, w, columns),
        ],
        out_specs=kept(roots, w, columns),
        out_shape=shape((roots, w, columns), F32),
        compiler_params=limit(16),
        cost_estimate=cost(3),
        name="root_terms",
    )(leaf_links, leaf_lower, leaf_lower, leaf_lower, leaf_solved)

    sep_forward = pl.pallas_call(
        separator_operator_kernel,
        in_specs=[whole()] * 2 + [ANY],
        out_specs=whole(),
        out_shape=shape((6 * w, 2 * w), BF16),
        compiler_params=limit(16),
        cost_estimate=cost(0.5),
        name="separator_operator",
    )(separator_lower_inverse, separator_lower_blocks, leaf_solved)

    sep_right, mine, theirs = pl.pallas_call(
        separator_kernel,
        in_specs=[whole(SMEM), whole(SMEM)] + [whole()] * 6,
        out_specs=[whole()] * 3,
        out_shape=[
            shape((2 * w, columns), BF16),
            shape((roots, w, half), F32),
            shape((roots, w, half), F32),
        ],
        scratch_shapes=[VMEM((roots, w, columns), F32)],
        compiler_params=limit(16),
        cost_estimate=cost(2),
        name="separator_forward",
    )(
        sep_links,
        place,
        separator_right_sides,
        sep_forward,
        own,
        far_sum,
        near_sum,
        root_pending,
    )

    other = swapped(theirs)
    sep_mine, sep_pack = pl.pallas_call(
        separator_part_kernel,
        in_specs=[smem] * 2 + [whole()] * 4,
        out_specs=[whole()] * 2,
        out_shape=[half_block, shape((roots + 1, w, half), F32)],
        compiler_params=limit(16),
        cost_estimate=cost(0.7),
        name="separator_part",
    )(
        sep_links,
        place,
        separator_lower_inverse,
        separator_upper_inverse,
        sep_upper,
        sep_right,
    )
    other_pack = swapped(sep_pack)
    pieces = [mine[j] + other[j] for j in range(4)]
    forward, backward = pl.pallas_call(
        root_sweeps_kernel,
        in_specs=[whole()] * 4 + [ANY],
        out_specs=[whole()] * 2,
        out_shape=[shape((roots * w, roots * w), F32)] * 2,
        compiler_params=limit(16),
        cost_estimate=cost(2.3),
        name="root_sweeps",
    )(root_lower_inverse, root_upper_inverse, root_lower, root_upper, pieces[1])
    arrived = [crossed(pieces[j], j) for j in (3, 2, 1)]
    arrived, forward, backward = lax.optimization_barrier((arrived, forward, backward))
    total = pieces[0] + arrived[0] + arrived[1] + arrived[2]

    root_operator, root_right = pl.pallas_call(
        root_operator_kernel,
        in_specs=[whole()] * 2 + [ANY],
        out_specs=[whole()] * 2,
        out_shape=[
            shape((2 * roots * w, 2 * roots * w), BF16),
            shape((2 * roots * w, roots * w), BF16),
        ],
        compiler_params=limit(16),
        cost_estimate=cost(1),
        name="root_operator",
    )(forward, backward, total)

    bit = 4
    while bit < peers:
        arrived = crossed(total, bit)
        if bit == 4:
            arrived, root_operator = lax.optimization_barrier((arrived, root_operator))
        total = total + arrived
        bit *= 2
    sep_backward = pl.pallas_call(
        separator_factors_kernel,
        in_specs=[whole()] * 3,
        out_specs=whole(),
        out_shape=shape((2, 2 * w, 2 * roots * w), BF16),
        compiler_params=limit(16),
        cost_estimate=cost(0.5),
        name="separator_factors",
    )(sep_pack, other_pack, root_right)
    others = [crossed(total, j) for j in (3, 2, 1)]

    solution_half, sep_own, sep_other, own_again, other_again = pl.pallas_call(
        root_kernel,
        in_specs=[smem] + [whole()] * 9,
        out_specs=[whole()] * 5,
        out_shape=[shape((roots + 1, w, half), F32)] + [half_block] * 4,
        scratch_shapes=[VMEM((2 * roots * w, half), BF16)],
        compiler_params=limit(16),
        cost_estimate=cost(2),
        name="root_solve",
    )(
        place,
        root_rhs,
        root_operator,
        *others,
        total,
        sep_backward,
        sep_mine,
        other_pack,
    )

    far_rows = shifted(sep_own, peers // 2)
    far_other_rows = shifted(sep_other, peers // 2, 1)
    near_rows = shifted(own_again, 1)
    near_other_rows = shifted(other_again, 1, 1)
    other_half = swapped(solution_half)

    leaf_operator = pl.pallas_call(
        leaf_operator_kernel,
        grid=(leaves // batch,),
        in_specs=[leafwise(batch, w, w), link(batch, 0, w), ANY],
        out_specs=leafwise(batch, 2 * w, 2 * w),
        out_shape=shape((leaves, 2 * w, 2 * w), BF16),
        compiler_params=limit(16),
        cost_estimate=cost(1),
        name="leaf_operators",
    )(leaf_upper_inverse, leaf_upper, sep_own)

    leaf_part, root_sol, separator_solution_rows = pl.pallas_call(
        leaf_root_part_kernel,
        grid=(leaves // batch,),
        in_specs=[
            smem,
            smem,
            link(batch, 1, w),
            link(batch, 2, w),
            link(batch, 3, w),
            leafwise(batch, w, w),
            leafwise(batch, w, columns),
            kept(roots + 1, w, half),
            kept(roots + 1, w, half),
            kept(w, half),
        ],
        out_specs=[
            leafwise(batch, w, columns),
            kept(roots, w, columns),
            kept(1, w, columns),
        ],
        out_shape=[
            shape((leaves, w, columns), F32),
            shape((roots, w, columns), F32),
            shape((1, w, columns), F32),
        ],
        scratch_shapes=[VMEM((roots, 2 * w, columns), BF16)],
        compiler_params=limit(16),
        cost_estimate=cost(3),
        name="leaf_root_part",
    )(
        leaf_links,
        place,
        leaf_upper,
        leaf_upper,
        leaf_upper,
        leaf_upper_inverse,
        leaf_solved,
        solution_half,
        other_half,
        sep_own,
    )

    leaf_sol = pl.pallas_call(
        leaf_final_kernel,
        in_specs=[smem] * 2 + [whole()] * 8,
        out_specs=ANY,
        out_shape=shape((leaves, w, columns), F32),
        scratch_shapes=[
            VMEM((3, 2 * w, columns), BF16),
            VMEM((leaves, w, columns), F32),
            pltpu.SemaphoreType.DMA((leaves // 2,)),
        ],
        compiler_params=limit(16),
        cost_estimate=cost(2),
        name="leaf_backward",
    )(
        leaf_links,
        place,
        leaf_operator,
        leaf_part,
        sep_own,
        other_half,
        near_rows,
        far_rows,
        near_other_rows,
        far_other_rows,
    )
    return (leaf_sol, separator_solution_rows, root_sol)


def solution(mesh):
    by_device = P(("groups", "grid", "layer"))
    by_group = P("groups")
    return jax.shard_map(
        per_device,
        mesh=mesh,
        in_specs=(by_device,) * 12 + (by_group,) * 5,
        out_specs=(by_device, by_device, by_group),
        check_vma=False,
    )
```

```python
import functools

import jax
import jax.numpy as jnp
from jax import lax
from jax.experimental import pallas as pl
from jax.experimental.pallas import tpu as pltpu
from jax.sharding import PartitionSpec as P

VMEM = pltpu.VMEM
SMEM = pltpu.SMEM
F32 = jnp.float32
BF16 = jnp.bfloat16


def parts_of(x):
    high = x.astype(BF16)
    low = (x - high.astype(F32)).astype(BF16)
    return high, low


def as_left(x):
    high, low = parts_of(x)
    count = x.shape[1] // 128
    pieces = [slice(j * 128, j * 128 + 128) for j in range(count)]
    top = jnp.concatenate([high[:, s] for s in pieces for _ in range(2)], axis=1)
    bottom = jnp.concatenate([low[:, s] for s in pieces for _ in range(2)], axis=1)
    return jnp.concatenate([top, bottom], axis=0)


def as_right(x):
    high, low = parts_of(x)
    count = x.shape[0] // 128
    pieces = [slice(j * 128, j * 128 + 128) for j in range(count)]
    return jnp.concatenate([y[s] for s in pieces for y in (high, low)], axis=0)


def left_times(left, right):
    both = jnp.dot(left, right, preferred_element_type=F32)
    rows = left.shape[0] // 2
    return both[:rows] + both[rows:]


def times(a, b):
    return left_times(as_left(a), as_right(b))


def halves(is_first, mine, other):
    return jnp.where(is_first, mine, other), jnp.where(is_first, other, mine)


def cost(microseconds):
    return pl.CostEstimate(
        flops=int(microseconds * 1e9),
        bytes_accessed=int(microseconds * 3e6),
        transcendentals=0,
    )


def forward_leaf_kernel(links, rhs, inverse, first, own, far, near, pending):
    step = pl.program_id(0)

    @pl.when(step == 0)
    def _():
        pending[...] = jnp.zeros_like(pending)

    batch = rhs.shape[0]
    values = []
    for i in range(batch):
        values.append(times(inverse[i], rhs[i]))
    for i in range(batch):
        pending[links[0, step * batch + i]] += times(first[i, 0], values[i])

    @pl.when(step == pl.num_programs(0) - 1)
    def _():
        own[...] = pending[0]
        near[...] = pending[1]
        far[...] = pending[2]


def root_terms_kernel(links, rhs, inverse, one, two, three, after, solved, pending):
    step = pl.program_id(0)

    @pl.when(step == 0)
    def _():
        pending[...] = jnp.zeros_like(pending)

    batch = rhs.shape[0]
    for i in range(batch):
        value = times(inverse[i], rhs[i])
        solved[i] = value
        blocks = jnp.concatenate([one[i, 0], two[i, 0], three[i, 0]], axis=0)
        terms = times(blocks, value)
        for n in range(3):
            slot = links[n + 1, step * batch + i] - 3
            pending[slot] += terms[n * 128 : n * 128 + 128]


def root_sweeps_kernel(lower_inverse, upper_inverse, lower, upper, after, forward, backward):
    count = lower_inverse.shape[0]
    w = lower_inverse.shape[1]
    forward[...] = jnp.zeros_like(forward)
    backward[...] = jnp.zeros_like(backward)
    for step in range(count):
        r = step
        here = slice(r * w, r * w + w)
        forward[here, here] = lower_inverse[r]
        if step > 0:
            done = slice(0, r * w)
            inner = times(lower[here, done], forward[done, done])
            forward[here, done] = -times(lower_inverse[r], inner)
        r = count - 1 - step
        here = slice(r * w, r * w + w)
        backward[here, here] = upper_inverse[r]
        if step > 0:
            done = slice((r + 1) * w, count * w)
            inner = times(upper[here, done], backward[done, done])
            backward[here, done] = -times(upper_inverse[r], inner)


def root_operator_kernel(forward, backward, after, root_operator, root_right):
    w = 128
    size = forward.shape[0]
    for r in range(0, size, w):
        block = times(backward[r : r + w, r:], forward[r:, :])
        root_right[2 * r : 2 * r + 2 * w, :] = as_right(block)
        left = as_left(block)
        root_operator[r : r + w, :] = left[:w]
        root_operator[size + r : size + r + w, :] = left[w:]


def separator_operator_kernel(lower_inverse, lower, after, forward):
    blocks = jnp.concatenate([lower[0, n] for n in range(3)], axis=0)
    forward[...] = as_left(times(blocks, lower_inverse[0]))


def separator_kernel(
    links, place, rhs, operator, own, far, near, root_pending, right, mine, theirs, sums
):
    right[...] = as_right(rhs[0] - own[...] - near[...] - far[...])
    terms = left_times(operator[...], right[...])
    sums[...] = root_pending[...]
    for n in range(3):
        sums[links[n]] += terms[n * 128 : n * 128 + 128]
    position = place[0]
    is_first = place[1] == 0
    for j in range(4):
        block = sums[position ^ j]
        first, second = block[:, :128], block[:, 128:]
        mine[j] = jnp.where(is_first, first, second)
        theirs[j] = jnp.where(is_first, second, first)


def separator_part_kernel(
    links, place, lower_inverse, upper_inverse, upper, right, mine, pack
):
    blocks = jnp.concatenate([upper[0, n] for n in range(3)], axis=1)
    back = times(upper_inverse[0], blocks)
    last = pack.shape[0] - 1
    pack[...] = jnp.zeros_like(pack)
    for n in range(3):
        pack[links[n]] = back[:, n * 128 : n * 128 + 128]
    operator = as_left(times(upper_inverse[0], lower_inverse[0]))
    part = left_times(operator, right[...])
    mine[...], pack[last] = halves(place[1] == 0, part[:, :128], part[:, 128:])


def separator_factors_kernel(pack, other, root_right, backward):
    for i, blocks in enumerate((pack, other)):
        row = jnp.concatenate([blocks[r] for r in range(blocks.shape[0] - 1)], axis=1)
        backward[i] = as_left(left_times(as_left(row), root_right[...]))


def root_kernel(
    place,
    rhs,
    operator,
    three,
    two,
    one,
    own,
    backward,
    part,
    other_pack,
    out,
    sep_own,
    sep_other,
    own_again,
    other_again,
    pending,
):
    count, w = rhs.shape[0], rhs.shape[1]
    position = place[0]
    is_first = place[1] == 0
    for j, piece in enumerate((own, one, two, three)):
        root = position ^ j
        side = rhs[root]
        side = jnp.where(is_first, side[:, :128], side[:, 128:])
        pending[pl.ds(pl.multiple_of(root * 2 * w, 2 * w), 2 * w), :] = as_right(
            side - piece[...]
        )
    solution = left_times(operator[...], pending[...])
    for r in range(count):
        out[r] = solution[r * w : r * w + w]
    sep_own[...] = part[...] - left_times(backward[0], pending[...])
    sep_other[...] = other_pack[count] - left_times(backward[1], pending[...])
    out[count] = sep_other[...]
    own_again[...] = sep_own[...]
    other_again[...] = sep_other[...]


def leaf_operator_kernel(inverse, first, after, operator):
    for i in range(inverse.shape[0]):
        operator[i] = as_left(times(inverse[i], first[i, 0]))


def leaf_root_part_kernel(
    links,
    place,
    one,
    two,
    three,
    inverse,
    solved,
    mine,
    other,
    sep_own,
    part,
    root_sol,
    sep_rows,
    right,
):
    step = pl.program_id(0)
    count = root_sol.shape[0]

    @pl.when(step == 0)
    def _():
        is_first = place[1] == 0
        for r in range(count):
            root_sol[r, :, :128], root_sol[r, :, 128:] = halves(is_first, mine[r], other[r])
            right[r] = as_right(root_sol[r])
        sep_rows[0, :, :128], sep_rows[0, :, 128:] = halves(is_first, sep_own[...], other[count])

    batch = solved.shape[0]
    rests = []
    for i in range(batch):
        leaf = step * batch + i
        blocks = jnp.concatenate([one[i, 0], two[i, 0], three[i, 0]], axis=1)
        linked = jnp.concatenate([right[links[n, leaf] - 3] for n in (1, 2, 3)], axis=0)
        rests.append(solved[i] - left_times(as_left(blocks), linked))
    for i in range(batch):
        part[i] = times(inverse[i], rests[i])


def leaf_final_kernel(
    links,
    place,
    operator,
    part,
    own,
    other,
    near,
    far,
    near_other,
    far_other,
    out,
    seps,
    ready,
    sems,
):
    is_first = place[1] == 0
    last = other[other.shape[0] - 1]
    for t, (a, b) in enumerate(
        ((own[...], last), (near[...], near_other[...]), (far[...], far_other[...]))
    ):
        first, second = halves(is_first, a, b)
        seps[t, :, :128] = as_right(first)
        seps[t, :, 128:] = as_right(second)
    count = part.shape[0]
    copies = []
    for i in range(count):
        ready[i] = part[i] - left_times(operator[i], seps[links[0, i]])
        if i % 2 == 1:
            pair = pl.ds(i - 1, 2)
            copy = pltpu.make_async_copy(ready.at[pair], out.at[pair], sems.at[i // 2])
            copy.start()
            copies.append(copy)
    for copy in copies:
        copy.wait()


def whole(memory=VMEM):
    return pl.BlockSpec(memory_space=memory)


ANY = pl.BlockSpec(memory_space=pl.ANY)


def limit(megabytes):
    return pltpu.CompilerParams(vmem_limit_bytes=megabytes * 1024 * 1024)


def leafwise(batch, *tail):
    return pl.BlockSpec((batch,) + tail, lambda k: (k,) + (0,) * len(tail))


def link(batch, n, w):
    return pl.BlockSpec((batch, 1, w, w), lambda k: (k, n, 0, 0))


def kept(*shape):
    return pl.BlockSpec(shape, lambda k: (0,) * len(shape))


def per_device(
    leaf_rhs,
    leaf_lower_inverse,
    leaf_upper_inverse,
    leaf_lower,
    leaf_upper,
    leaf_rows,
    separator_right_sides,
    separator_lower_inverse,
    separator_upper_inverse,
    separator_lower_blocks,
    sep_upper,
    sep_rows,
    root_rhs,
    root_lower_inverse,
    root_upper_inverse,
    root_lower,
    root_upper,
):
    peers = lax.axis_size("grid")
    leaves, w, columns = leaf_rhs.shape
    roots = root_rhs.shape[0]
    half = columns // 2
    batch = leaves // 2
    position = lax.axis_index("grid") % 4
    core = lax.axis_index("layer")
    place = jnp.stack([position, core]).astype(jnp.int32)
    leaf_links = leaf_rows.T
    sep_links = sep_rows.reshape(-1)

    def shifted(x, by, to_other=0):
        pairs = [
            (2 * i + c, 2 * ((i + by) % peers) + (c ^ to_other))
            for i in range(peers)
            for c in range(2)
        ]
        return lax.ppermute(x, ("grid", "layer"), pairs)

    def crossed(x, bit):
        return lax.ppermute(x, "grid", [(i, i ^ bit) for i in range(peers)])

    def swapped(x):
        return lax.ppermute(x, "layer", [(0, 1), (1, 0)])

    shape = jax.ShapeDtypeStruct
    half_block = shape((w, half), F32)
    smem = whole(SMEM)

    own, far, near = pl.pallas_call(
        forward_leaf_kernel,
        grid=(leaves // batch,),
        in_specs=[
            whole(SMEM),
            leafwise(batch, w, columns),
            leafwise(batch, w, w),
            link(batch, 0, w),
        ],
        out_specs=[kept(w, columns)] * 3,
        out_shape=[shape((w, columns), F32)] * 3,
        scratch_shapes=[VMEM((3, w, columns), F32)],
        compiler_params=limit(56),
        cost_estimate=cost(4),
        name="leaf_forward",
    )(leaf_links, leaf_rhs, leaf_lower_inverse, leaf_lower)

    far_sum = shifted(far, -(peers // 2))
    near_sum = shifted(near, -1)

    leaf_solved, root_pending = pl.pallas_call(
        root_terms_kernel,
        grid=(leaves // batch,),
        in_specs=[
            smem,
            leafwise(batch, w, columns),
            leafwise(batch, w, w),
            link(batch, 1, w),
            link(batch, 2, w),
            link(batch, 3, w),
            ANY,
        ],
        out_specs=[leafwise(batch, w, columns), kept(roots, w, columns)],
        out_shape=[shape((leaves, w, columns), F32), shape((roots, w, columns), F32)],
        compiler_params=limit(16),
        cost_estimate=cost(3),
        name="root_terms",
    )(leaf_links, leaf_rhs, leaf_lower_inverse, leaf_lower, leaf_lower, leaf_lower, own)

    sep_forward = pl.pallas_call(
        separator_operator_kernel,
        in_specs=[whole()] * 2 + [ANY],
        out_specs=whole(),
        out_shape=shape((6 * w, 2 * w), BF16),
        compiler_params=limit(16),
        cost_estimate=cost(0.5),
        name="separator_operator",
    )(separator_lower_inverse, separator_lower_blocks, own)

    sep_right, mine, theirs = pl.pallas_call(
        separator_kernel,
        in_specs=[whole(SMEM), whole(SMEM)] + [whole()] * 6,
        out_specs=[whole()] * 3,
        out_shape=[
            shape((2 * w, columns), BF16),
            shape((roots, w, half), F32),
            shape((roots, w, half), F32),
        ],
        scratch_shapes=[VMEM((roots, w, columns), F32)],
        compiler_params=limit(16),
        cost_estimate=cost(2),
        name="separator_forward",
    )(
        sep_links,
        place,
        separator_right_sides,
        sep_forward,
        own,
        far_sum,
        near_sum,
        root_pending,
    )

    other = swapped(theirs)
    sep_mine, sep_pack = pl.pallas_call(
        separator_part_kernel,
        in_specs=[smem] * 2 + [whole()] * 4,
        out_specs=[whole()] * 2,
        out_shape=[half_block, shape((roots + 1, w, half), F32)],
        compiler_params=limit(16),
        cost_estimate=cost(0.7),
        name="separator_part",
    )(
        sep_links,
        place,
        separator_lower_inverse,
        separator_upper_inverse,
        sep_upper,
        sep_right,
    )
    other_pack = swapped(sep_pack)
    pieces = [mine[j] + other[j] for j in range(4)]
    forward, backward = pl.pallas_call(
        root_sweeps_kernel,
        in_specs=[whole()] * 4 + [ANY],
        out_specs=[whole()] * 2,
        out_shape=[shape((roots * w, roots * w), F32)] * 2,
        compiler_params=limit(16),
        cost_estimate=cost(2.3),
        name="root_sweeps",
    )(root_lower_inverse, root_upper_inverse, root_lower, root_upper, pieces[1])
    arrived = [crossed(pieces[j], j) for j in (3, 2, 1)]
    arrived, forward, backward = lax.optimization_barrier((arrived, forward, backward))
    total = pieces[0] + arrived[0] + arrived[1] + arrived[2]

    root_operator, root_right = pl.pallas_call(
        root_operator_kernel,
        in_specs=[whole()] * 2 + [ANY],
        out_specs=[whole()] * 2,
        out_shape=[
            shape((2 * roots * w, 2 * roots * w), BF16),
            shape((2 * roots * w, roots * w), BF16),
        ],
        compiler_params=limit(16),
        cost_estimate=cost(1),
        name="root_operator",
    )(forward, backward, total)

    bit = 4
    while bit < peers:
        arrived = crossed(total, bit)
        if bit == 4:
            arrived, root_operator = lax.optimization_barrier((arrived, root_operator))
        total = total + arrived
        bit *= 2
    sep_backward = pl.pallas_call(
        separator_factors_kernel,
        in_specs=[whole()] * 3,
        out_specs=whole(),
        out_shape=shape((2, 2 * w, 2 * roots * w), BF16),
        compiler_params=limit(16),
        cost_estimate=cost(0.5),
        name="separator_factors",
    )(sep_pack, other_pack, root_right)
    others = [crossed(total, j) for j in (3, 2, 1)]

    solution_half, sep_own, sep_other, own_again, other_again = pl.pallas_call(
        root_kernel,
        in_specs=[smem] + [whole()] * 9,
        out_specs=[whole()] * 5,
        out_shape=[shape((roots + 1, w, half), F32)] + [half_block] * 4,
        scratch_shapes=[VMEM((2 * roots * w, half), BF16)],
        compiler_params=limit(16),
        cost_estimate=cost(2),
        name="root_solve",
    )(
        place,
        root_rhs,
        root_operator,
        *others,
        total,
        sep_backward,
        sep_mine,
        other_pack,
    )

    far_rows = shifted(sep_own, peers // 2)
    far_other_rows = shifted(sep_other, peers // 2, 1)
    near_rows = shifted(own_again, 1)
    near_other_rows = shifted(other_again, 1, 1)
    other_half = swapped(solution_half)

    leaf_operator = pl.pallas_call(
        leaf_operator_kernel,
        grid=(leaves // batch,),
        in_specs=[leafwise(batch, w, w), link(batch, 0, w), ANY],
        out_specs=leafwise(batch, 2 * w, 2 * w),
        out_shape=shape((leaves, 2 * w, 2 * w), BF16),
        compiler_params=limit(16),
        cost_estimate=cost(1),
        name="leaf_operators",
    )(leaf_upper_inverse, leaf_upper, sep_own)

    leaf_part, root_sol, separator_solution_rows = pl.pallas_call(
        leaf_root_part_kernel,
        grid=(leaves // batch,),
        in_specs=[
            smem,
            smem,
            link(batch, 1, w),
            link(batch, 2, w),
            link(batch, 3, w),
            leafwise(batch, w, w),
            leafwise(batch, w, columns),
            kept(roots + 1, w, half),
            kept(roots + 1, w, half),
            kept(w, half),
        ],
        out_specs=[
            leafwise(batch, w, columns),
            kept(roots, w, columns),
            kept(1, w, columns),
        ],
        out_shape=[
            shape((leaves, w, columns), F32),
            shape((roots, w, columns), F32),
            shape((1, w, columns), F32),
        ],
        scratch_shapes=[VMEM((roots, 2 * w, columns), BF16)],
        compiler_params=limit(16),
        cost_estimate=cost(3),
        name="leaf_root_part",
    )(
        leaf_links,
        place,
        leaf_upper,
        leaf_upper,
        leaf_upper,
        leaf_upper_inverse,
        leaf_solved,
        solution_half,
        other_half,
        sep_own,
    )

    leaf_sol = pl.pallas_call(
        leaf_final_kernel,
        in_specs=[smem] * 2 + [whole()] * 8,
        out_specs=ANY,
        out_shape=shape((leaves, w, columns), F32),
        scratch_shapes=[
            VMEM((3, 2 * w, columns), BF16),
            VMEM((leaves, w, columns), F32),
            pltpu.SemaphoreType.DMA((leaves // 2,)),
        ],
        compiler_params=limit(16),
        cost_estimate=cost(2),
        name="leaf_backward",
    )(
        leaf_links,
        place,
        leaf_operator,
        leaf_part,
        sep_own,
        other_half,
        near_rows,
        far_rows,
        near_other_rows,
        far_other_rows,
    )
    return (leaf_sol, separator_solution_rows, root_sol)


def solution(mesh):
    by_device = P(("groups", "grid", "layer"))
    by_group = P("groups")
    return jax.shard_map(
        per_device,
        mesh=mesh,
        in_specs=(by_device,) * 12 + (by_group,) * 5,
        out_specs=(by_device, by_device, by_group),
        check_vma=False,
    )
```

```python
import functools

import jax
import jax.numpy as jnp
from jax import lax
from jax.experimental import pallas as pl
from jax.experimental.pallas import tpu as pltpu
from jax.sharding import PartitionSpec as P

VMEM = pltpu.VMEM
SMEM = pltpu.SMEM
F32 = jnp.float32
BF16 = jnp.bfloat16


def parts_of(x):
    high = x.astype(BF16)
    low = (x - high.astype(F32)).astype(BF16)
    return high, low


def as_left(x):
    high, low = parts_of(x)
    count = x.shape[1] // 128
    pieces = [slice(j * 128, j * 128 + 128) for j in range(count)]
    top = jnp.concatenate([high[:, s] for s in pieces for _ in range(2)], axis=1)
    bottom = jnp.concatenate([low[:, s] for s in pieces for _ in range(2)], axis=1)
    return jnp.concatenate([top, bottom], axis=0)


def as_right(x):
    high, low = parts_of(x)
    count = x.shape[0] // 128
    pieces = [slice(j * 128, j * 128 + 128) for j in range(count)]
    return jnp.concatenate([y[s] for s in pieces for y in (high, low)], axis=0)


def left_times(left, right):
    both = jnp.dot(left, right, preferred_element_type=F32)
    rows = left.shape[0] // 2
    return both[:rows] + both[rows:]


def times(a, b):
    return left_times(as_left(a), as_right(b))


def halves(is_first, mine, other):
    return jnp.where(is_first, mine, other), jnp.where(is_first, other, mine)


def cost(microseconds):
    return pl.CostEstimate(
        flops=int(microseconds * 1e9),
        bytes_accessed=int(microseconds * 3e6),
        transcendentals=0,
    )


def forward_leaf_kernel(links, rhs, inverse, first, own, far, near, pending):
    step = pl.program_id(0)

    @pl.when(step == 0)
    def _():
        pending[...] = jnp.zeros_like(pending)

    batch = rhs.shape[0]
    values = []
    for i in range(batch):
        values.append(times(inverse[i], rhs[i]))
    for i in range(batch):
        pending[links[0, step * batch + i]] += times(first[i, 0], values[i])

    @pl.when(step == pl.num_programs(0) - 1)
    def _():
        own[...] = pending[0]
        near[...] = pending[1]
        far[...] = pending[2]


def root_terms_kernel(links, rhs, inverse, one, two, three, after, solved, pending):
    step = pl.program_id(0)

    @pl.when(step == 0)
    def _():
        pending[...] = jnp.zeros_like(pending)

    batch = rhs.shape[0]
    for i in range(batch):
        value = times(inverse[i], rhs[i])
        solved[i] = value
        blocks = jnp.concatenate([one[i, 0], two[i, 0], three[i, 0]], axis=0)
        terms = times(blocks, value)
        for n in range(3):
            slot = links[n + 1, step * batch + i] - 3
            pending[slot] += terms[n * 128 : n * 128 + 128]


def root_sweeps_kernel(lower_inverse, upper_inverse, lower, upper, after, forward, backward):
    count = lower_inverse.shape[0]
    w = lower_inverse.shape[1]
    forward[...] = jnp.zeros_like(forward)
    backward[...] = jnp.zeros_like(backward)
    for step in range(count):
        r = step
        here = slice(r * w, r * w + w)
        forward[here, here] = lower_inverse[r]
        if step > 0:
            done = slice(0, r * w)
            inner = times(lower[here, done], forward[done, done])
            forward[here, done] = -times(lower_inverse[r], inner)
        r = count - 1 - step
        here = slice(r * w, r * w + w)
        backward[here, here] = upper_inverse[r]
        if step > 0:
            done = slice((r + 1) * w, count * w)
            inner = times(upper[here, done], backward[done, done])
            backward[here, done] = -times(upper_inverse[r], inner)


def root_operator_kernel(forward, backward, after, root_operator, root_right):
    w = 128
    size = forward.shape[0]
    for r in range(0, size, w):
        block = times(backward[r : r + w, r:], forward[r:, :])
        root_right[2 * r : 2 * r + 2 * w, :] = as_right(block)
        left = as_left(block)
        root_operator[r : r + w, :] = left[:w]
        root_operator[size + r : size + r + w, :] = left[w:]


def separator_operator_kernel(lower_inverse, lower, after, forward):
    blocks = jnp.concatenate([lower[0, n] for n in range(3)], axis=0)
    forward[...] = as_left(times(blocks, lower_inverse[0]))


def separator_kernel(
    links, place, rhs, operator, own, far, near, root_pending, right, mine, theirs, sums
):
    right[...] = as_right(rhs[0] - own[...] - near[...] - far[...])
    terms = left_times(operator[...], right[...])
    sums[...] = root_pending[...]
    for n in range(3):
        sums[links[n]] += terms[n * 128 : n * 128 + 128]
    position = place[0]
    is_first = place[1] == 0
    for j in range(4):
        block = sums[position ^ j]
        first, second = block[:, :128], block[:, 128:]
        mine[j] = jnp.where(is_first, first, second)
        theirs[j] = jnp.where(is_first, second, first)


def separator_part_kernel(
    links, place, lower_inverse, upper_inverse, upper, right, mine, pack
):
    blocks = jnp.concatenate([upper[0, n] for n in range(3)], axis=1)
    back = times(upper_inverse[0], blocks)
    last = pack.shape[0] - 1
    pack[...] = jnp.zeros_like(pack)
    for n in range(3):
        pack[links[n]] = back[:, n * 128 : n * 128 + 128]
    operator = as_left(times(upper_inverse[0], lower_inverse[0]))
    part = left_times(operator, right[...])
    mine[...], pack[last] = halves(place[1] == 0, part[:, :128], part[:, 128:])


def separator_factors_kernel(pack, other, root_right, backward):
    for i, blocks in enumerate((pack, other)):
        row = jnp.concatenate([blocks[r] for r in range(blocks.shape[0] - 1)], axis=1)
        backward[i] = as_left(left_times(as_left(row), root_right[...]))


def root_kernel(
    place,
    rhs,
    operator,
    three,
    two,
    one,
    own,
    backward,
    part,
    other_pack,
    out,
    sep_own,
    sep_other,
    own_again,
    other_again,
    pending,
):
    count, w = rhs.shape[0], rhs.shape[1]
    position = place[0]
    is_first = place[1] == 0
    for j, piece in enumerate((own, one, two, three)):
        root = position ^ j
        side = rhs[root]
        side = jnp.where(is_first, side[:, :128], side[:, 128:])
        pending[pl.ds(pl.multiple_of(root * 2 * w, 2 * w), 2 * w), :] = as_right(
            side - piece[...]
        )
    solution = left_times(operator[...], pending[...])
    for r in range(count):
        out[r] = solution[r * w : r * w + w]
    sep_own[...] = part[...] - left_times(backward[0], pending[...])
    sep_other[...] = other_pack[count] - left_times(backward[1], pending[...])
    out[count] = sep_other[...]
    own_again[...] = sep_own[...]
    other_again[...] = sep_other[...]


def leaf_operator_kernel(inverse, first, after, operator):
    for i in range(inverse.shape[0]):
        operator[i] = as_left(times(inverse[i], first[i, 0]))


def leaf_root_part_kernel(
    links,
    place,
    one,
    two,
    three,
    inverse,
    solved,
    mine,
    other,
    sep_own,
    part,
    root_sol,
    sep_rows,
    right,
):
    step = pl.program_id(0)
    count = root_sol.shape[0]

    @pl.when(step == 0)
    def _():
        is_first = place[1] == 0
        for r in range(count):
            root_sol[r, :, :128], root_sol[r, :, 128:] = halves(is_first, mine[r], other[r])
            right[r] = as_right(root_sol[r])
        sep_rows[0, :, :128], sep_rows[0, :, 128:] = halves(is_first, sep_own[...], other[count])

    batch = solved.shape[0]
    rests = []
    for i in range(batch):
        leaf = step * batch + i
        blocks = jnp.concatenate([one[i, 0], two[i, 0], three[i, 0]], axis=1)
        linked = jnp.concatenate([right[links[n, leaf] - 3] for n in (1, 2, 3)], axis=0)
        rests.append(solved[i] - left_times(as_left(blocks), linked))
    for i in range(batch):
        part[i] = times(inverse[i], rests[i])


def leaf_final_kernel(
    links,
    place,
    operator,
    part,
    own,
    other,
    near,
    far,
    near_other,
    far_other,
    out,
    seps,
    ready,
    sems,
):
    is_first = place[1] == 0
    last = other[other.shape[0] - 1]
    for t, (a, b) in enumerate(
        ((own[...], last), (near[...], near_other[...]), (far[...], far_other[...]))
    ):
        first, second = halves(is_first, a, b)
        seps[t, :, :128] = as_right(first)
        seps[t, :, 128:] = as_right(second)
    count = part.shape[0]
    copies = []
    for i in range(count):
        ready[i] = part[i] - left_times(operator[i], seps[links[0, i]])
        if i % 2 == 1:
            pair = pl.ds(i - 1, 2)
            copy = pltpu.make_async_copy(ready.at[pair], out.at[pair], sems.at[i // 2])
            copy.start()
            copies.append(copy)
    for copy in copies:
        copy.wait()


def whole(memory=VMEM):
    return pl.BlockSpec(memory_space=memory)


ANY = pl.BlockSpec(memory_space=pl.ANY)


def limit(megabytes):
    return pltpu.CompilerParams(vmem_limit_bytes=megabytes * 1024 * 1024)


def leafwise(batch, *tail):
    return pl.BlockSpec((batch,) + tail, lambda k: (k,) + (0,) * len(tail))


def link(batch, n, w):
    return pl.BlockSpec((batch, 1, w, w), lambda k: (k, n, 0, 0))


def kept(*shape):
    return pl.BlockSpec(shape, lambda k: (0,) * len(shape))


def per_device(
    leaf_rhs,
    leaf_lower_inverse,
    leaf_upper_inverse,
    leaf_lower,
    leaf_upper,
    leaf_rows,
    separator_right_sides,
    separator_lower_inverse,
    separator_upper_inverse,
    separator_lower_blocks,
    sep_upper,
    sep_rows,
    root_rhs,
    root_lower_inverse,
    root_upper_inverse,
    root_lower,
    root_upper,
):
    peers = lax.axis_size("grid")
    leaves, w, columns = leaf_rhs.shape
    roots = root_rhs.shape[0]
    half = columns // 2
    batch = leaves // 2
    position = lax.axis_index("grid") % 4
    core = lax.axis_index("layer")
    place = jnp.stack([position, core]).astype(jnp.int32)
    leaf_links = leaf_rows.T
    sep_links = sep_rows.reshape(-1)

    def shifted(x, by, to_other=0):
        pairs = [
            (2 * i + c, 2 * ((i + by) % peers) + (c ^ to_other))
            for i in range(peers)
            for c in range(2)
        ]
        return lax.ppermute(x, ("grid", "layer"), pairs)

    def crossed(x, bit):
        return lax.ppermute(x, "grid", [(i, i ^ bit) for i in range(peers)])

    def swapped(x):
        return lax.ppermute(x, "layer", [(0, 1), (1, 0)])

    shape = jax.ShapeDtypeStruct
    half_block = shape((w, half), F32)
    smem = whole(SMEM)

    own, far, near = pl.pallas_call(
        forward_leaf_kernel,
        grid=(leaves // batch,),
        in_specs=[
            whole(SMEM),
            leafwise(batch, w, columns),
            leafwise(batch, w, w),
            link(batch, 0, w),
        ],
        out_specs=[kept(w, columns)] * 3,
        out_shape=[shape((w, columns), F32)] * 3,
        scratch_shapes=[VMEM((3, w, columns), F32)],
        compiler_params=limit(56),
        cost_estimate=cost(4),
        name="leaf_forward",
    )(leaf_links, leaf_rhs, leaf_lower_inverse, leaf_lower)

    far_sum = shifted(far, -(peers // 2))
    near_sum = shifted(near, -1)

    leaf_solved, root_pending = pl.pallas_call(
        root_terms_kernel,
        grid=(leaves // batch,),
        in_specs=[
            smem,
            leafwise(batch, w, columns),
            leafwise(batch, w, w),
            link(batch, 1, w),
            link(batch, 2, w),
            link(batch, 3, w),
            ANY,
        ],
        out_specs=[leafwise(batch, w, columns), kept(roots, w, columns)],
        out_shape=[shape((leaves, w, columns), F32), shape((roots, w, columns), F32)],
        compiler_params=limit(16),
        cost_estimate=cost(3),
        name="root_terms",
    )(leaf_links, leaf_rhs, leaf_lower_inverse, leaf_lower, leaf_lower, leaf_lower, own)

    sep_forward = pl.pallas_call(
        separator_operator_kernel,
        in_specs=[whole()] * 2 + [ANY],
        out_specs=whole(),
        out_shape=shape((6 * w, 2 * w), BF16),
        compiler_params=limit(16),
        cost_estimate=cost(0.5),
        name="separator_operator",
    )(separator_lower_inverse, separator_lower_blocks, own)

    sep_right, mine, theirs = pl.pallas_call(
        separator_kernel,
        in_specs=[whole(SMEM), whole(SMEM)] + [whole()] * 6,
        out_specs=[whole()] * 3,
        out_shape=[
            shape((2 * w, columns), BF16),
            shape((roots, w, half), F32),
            shape((roots, w, half), F32),
        ],
        scratch_shapes=[VMEM((roots, w, columns), F32)],
        compiler_params=limit(16),
        cost_estimate=cost(2),
        name="separator_forward",
    )(
        sep_links,
        place,
        separator_right_sides,
        sep_forward,
        own,
        far_sum,
        near_sum,
        root_pending,
    )

    other = swapped(theirs)
    sep_mine, sep_pack = pl.pallas_call(
        separator_part_kernel,
        in_specs=[smem] * 2 + [whole()] * 4,
        out_specs=[whole()] * 2,
        out_shape=[half_block, shape((roots + 1, w, half), F32)],
        compiler_params=limit(16),
        cost_estimate=cost(0.7),
        name="separator_part",
    )(
        sep_links,
        place,
        separator_lower_inverse,
        separator_upper_inverse,
        sep_upper,
        sep_right,
    )
    other_pack = swapped(sep_pack)
    pieces = [mine[j] + other[j] for j in range(4)]
    forward, backward = pl.pallas_call(
        root_sweeps_kernel,
        in_specs=[whole()] * 4 + [ANY],
        out_specs=[whole()] * 2,
        out_shape=[shape((roots * w, roots * w), F32)] * 2,
        compiler_params=limit(16),
        cost_estimate=cost(2.3),
        name="root_sweeps",
    )(root_lower_inverse, root_upper_inverse, root_lower, root_upper, pieces[1])
    arrived = [crossed(pieces[j], j) for j in (3, 2, 1)]
    arrived, forward, backward = lax.optimization_barrier((arrived, forward, backward))
    total = pieces[0] + arrived[0] + arrived[1] + arrived[2]

    root_operator, root_right = pl.pallas_call(
        root_operator_kernel,
        in_specs=[whole()] * 2 + [ANY],
        out_specs=[whole()] * 2,
        out_shape=[
            shape((2 * roots * w, 2 * roots * w), BF16),
            shape((2 * roots * w, roots * w), BF16),
        ],
        compiler_params=limit(16),
        cost_estimate=cost(1),
        name="root_operator",
    )(forward, backward, total)

    bit = 4
    while bit < peers:
        arrived = crossed(total, bit)
        if bit == 4:
            arrived, root_operator = lax.optimization_barrier((arrived, root_operator))
        total = total + arrived
        bit *= 2
    sep_backward = pl.pallas_call(
        separator_factors_kernel,
        in_specs=[whole()] * 3,
        out_specs=whole(),
        out_shape=shape((2, 2 * w, 2 * roots * w), BF16),
        compiler_params=limit(16),
        cost_estimate=cost(0.5),
        name="separator_factors",
    )(sep_pack, other_pack, root_right)
    others = [crossed(total, j) for j in (3, 2, 1)]

    solution_half, sep_own, sep_other, own_again, other_again = pl.pallas_call(
        root_kernel,
        in_specs=[smem] + [whole()] * 9,
        out_specs=[whole()] * 5,
        out_shape=[shape((roots + 1, w, half), F32)] + [half_block] * 4,
        scratch_shapes=[VMEM((2 * roots * w, half), BF16)],
        compiler_params=limit(16),
        cost_estimate=cost(2),
        name="root_solve",
    )(
        place,
        root_rhs,
        root_operator,
        *others,
        total,
        sep_backward,
        sep_mine,
        other_pack,
    )

    far_rows = shifted(sep_own, peers // 2)
    far_other_rows = shifted(sep_other, peers // 2, 1)
    near_rows = shifted(own_again, 1)
    near_other_rows = shifted(other_again, 1, 1)
    other_half = swapped(solution_half)

    leaf_operator = pl.pallas_call(
        leaf_operator_kernel,
        grid=(leaves // batch,),
        in_specs=[leafwise(batch, w, w), link(batch, 0, w), ANY],
        out_specs=leafwise(batch, 2 * w, 2 * w),
        out_shape=shape((leaves, 2 * w, 2 * w), BF16),
        compiler_params=limit(16),
        cost_estimate=cost(1),
        name="leaf_operators",
    )(leaf_upper_inverse, leaf_upper, total)

    leaf_part, root_sol, separator_solution_rows = pl.pallas_call(
        leaf_root_part_kernel,
        grid=(leaves // batch,),
        in_specs=[
            smem,
            smem,
            link(batch, 1, w),
            link(batch, 2, w),
            link(batch, 3, w),
            leafwise(batch, w, w),
            leafwise(batch, w, columns),
            kept(roots + 1, w, half),
            kept(roots + 1, w, half),
            kept(w, half),
        ],
        out_specs=[
            leafwise(batch, w, columns),
            kept(roots, w, columns),
            kept(1, w, columns),
        ],
        out_shape=[
            shape((leaves, w, columns), F32),
            shape((roots, w, columns), F32),
            shape((1, w, columns), F32),
        ],
        scratch_shapes=[VMEM((roots, 2 * w, columns), BF16)],
        compiler_params=limit(16),
        cost_estimate=cost(3),
        name="leaf_root_part",
    )(
        leaf_links,
        place,
        leaf_upper,
        leaf_upper,
        leaf_upper,
        leaf_upper_inverse,
        leaf_solved,
        solution_half,
        other_half,
        sep_own,
    )

    leaf_sol = pl.pallas_call(
        leaf_final_kernel,
        in_specs=[smem] * 2 + [whole()] * 8,
        out_specs=ANY,
        out_shape=shape((leaves, w, columns), F32),
        scratch_shapes=[
            VMEM((3, 2 * w, columns), BF16),
            VMEM((leaves, w, columns), F32),
            pltpu.SemaphoreType.DMA((leaves // 2,)),
        ],
        compiler_params=limit(16),
        cost_estimate=cost(2),
        name="leaf_backward",
    )(
        leaf_links,
        place,
        leaf_operator,
        leaf_part,
        sep_own,
        other_half,
        near_rows,
        far_rows,
        near_other_rows,
        far_other_rows,
    )
    return (leaf_sol, separator_solution_rows, root_sol)


def solution(mesh):
    by_device = P(("groups", "grid", "layer"))
    by_group = P("groups")
    return jax.shard_map(
        per_device,
        mesh=mesh,
        in_specs=(by_device,) * 12 + (by_group,) * 5,
        out_specs=(by_device, by_device, by_group),
        check_vma=False,
    )
```
